32 devices in a mesh: seq: 16 (over z, x, core), head: 2 (over y).
Axes of the slice: x: 2, y: 2, z: 4, core: 2. Of those that a mesh axis runs over, the one named last changes fastest.
Arguments:
- projected: float32 [4096, 2560], P(('seq', 'head')), may hold values from -6 to 6
- out_grads: float32 [4096, 2048], P(('seq', 'head')), may hold values from -6 to 6
- conv_weight: float32 [3, 2560], replicated, may hold values from -2.4 to 2.4
- doc_lengths: int32 [4], replicated, may hold values from 1 to 2048, 4096 in all
Outputs:
- grad_projected: float32 [4096, 2560], P(('seq', 'head'))
- grad_conv: float32 [3, 2560], replicated
The draws below stay inside these ranges and needn't reach their ends.
Inputs may be any that keep to these rules, and one draw needn't show every extreme that they name: `doc_lengths`: the 4 documents fill the 4096 tokens end to end; the longest holds exactly half of 4096 tokens.
All inputs are finite; a program needn't handle non-finite values.
Results may differ from the reference program's by a relative error of at most 0.0003.
Values sent between devices are 32-bit elements; how exact they have to be, the bound alone decides.
A program may use at most 128 MiB of HBM per device.

```python
import math
import jax
import jax.numpy as jnp
import numpy as np
from jax import lax

HEADS = 16
KEY_DIM = 16
HEAD_DIM = 128
CONV_TAPS = 3
TOKENS = 4096
NDOC = 4


def levels(own_key, dims, shards, low, top_value):
    gain = 1.0
    for axis_at, shards_of in shards:
        steps = jax.random.uniform(jax.random.fold_in(jax.random.fold_in(own_key, 6), axis_at), (shards_of,), jnp.float32, low / len(shards), top_value / len(shards))
        gain = gain * jnp.repeat(jnp.exp(steps), dims[axis_at] // shards_of).reshape((-1,) + (1,) * (len(dims) - 1 - axis_at))
    return gain


def split_up(count, total, limit, skew):
    loads = [(1 << 20) // math.isqrt(rank ** skew) + 1 for rank in range(2, count + 1)]
    rest, counts = total - limit - (count - 1), [1] * (count - 1)
    while rest > 0:
        movable = [i for i in range(count - 1) if counts[i] < limit]
        pool, remaining = sum([loads[i] for i in movable]), rest
        for i in movable:
            more = min(limit - counts[i], max(1, remaining * loads[i] // pool), rest)
            counts[i] = counts[i] + more
            rest = rest - more
    return np.array([limit] + counts)


def ragged_sizes(own_key, count, total, bound, slope):
    if count == 2:
        one = jax.random.randint(own_key, (), max(1, total - bound), min(bound, total - 1) + 1)
        return jnp.stack([one, total - one])
    lengths = jnp.asarray(split_up(count, total, bound, slope), jnp.int32)
    twos = (count - 1) // 2
    giver, receiver = lengths[1:1 + 2 * twos:2], lengths[2:2 + 2 * twos:2]
    margin = jnp.minimum(giver - 1, bound - receiver)
    shifted = jax.random.randint(jax.random.fold_in(own_key, 1), (twos,), 0, 1 << 20) % (margin + 1)
    lengths = lengths.at[1:1 + 2 * twos:2].set(giver - shifted).at[2:2 + 2 * twos:2].set(receiver + shifted)
    return lengths[jax.random.permutation(jax.random.fold_in(own_key, 2), count)]


def scatter_about(rng, shape, scale, bound, split=(), kind=jnp.bfloat16):
    entries = jax.random.normal(rng, shape, jnp.float32) * scale
    if len(split) > 0:
        entries = levels(rng, shape, split, -0.22, 0.18) * entries
    return jnp.clip(entries, min=-bound, max=bound).astype(kind)


def setup_inputs(seed: int = 0) -> dict:
    splits = jax.random.split(jax.random.key(seed), 5)
    projected = scatter_about(splits[0], (TOKENS, HEADS * (2 * KEY_DIM + HEAD_DIM)), 1.0, 6.0, ((0, 32),), jnp.float32)
    out_grads = scatter_about(splits[1], (TOKENS, HEADS * HEAD_DIM), 1.0, 6.0, ((0, 32),), jnp.float32)
    conv_weight = scatter_about(splits[2], (CONV_TAPS, HEADS * (2 * KEY_DIM + HEAD_DIM)), 0.6, 2.4, (), jnp.float32)
    doc_lengths = ragged_sizes(splits[3], NDOC, TOKENS, TOKENS // 2, 2).astype(jnp.int32)
    return dict(projected=projected, out_grads=out_grads, conv_weight=conv_weight, doc_lengths=doc_lengths)


HIGHEST = lax.Precision.HIGHEST

def feature_rows(matrix):
    key_size = matrix.shape[-1]
    upper_i, upper_j = np.triu_indices(key_size)
    factors = np.where(upper_i == upper_j, 1.0 / math.sqrt(2.0), 1.0)
    products = matrix[:, upper_i] * matrix[:, upper_j] * jnp.asarray(factors, dtype=jnp.float32)[None, :]
    constant = jnp.ones((matrix.shape[0], 1), jnp.float32)
    return jnp.concatenate([constant, matrix, products], axis=1)

def shift_rows(matrix, amount):
    return jnp.concatenate([jnp.zeros_like(matrix[:amount]), matrix[:-amount]], axis=0)

def head_attention(triple, begins):
    query_rows, key_rows, value_rows = triple
    total = query_rows.shape[0]
    span_len = 128
    pieces = total // span_len
    query_feat = feature_rows(query_rows)
    key_feat = feature_rows(key_rows)
    causal = jnp.arange(span_len)[:, None] >= jnp.arange(span_len)[None, :]

    def advance(carried, inputs):
        carry_state, carry_norm = carried
        query_blk, key_blk, value_blk, doc_blk, block_start = inputs
        allowed = (causal & (doc_blk[:, None] == doc_blk[None, :])).astype(jnp.float32)
        scores = jnp.dot(query_blk, key_blk.T, precision=HIGHEST) * allowed
        from_carry = (doc_blk < block_start).astype(jnp.float32)
        numerator = jnp.dot(scores, value_blk, precision=HIGHEST) + from_carry[:, None] * jnp.dot(query_blk, carry_state, precision=HIGHEST)
        denominator = lax.optimization_barrier(jnp.sum(scores, axis=1)) + from_carry * jnp.dot(query_blk, carry_norm, precision=HIGHEST)
        block_tail = (doc_blk == doc_blk[span_len - 1]).astype(jnp.float32)
        carry_keep = (doc_blk[span_len - 1] < block_start).astype(jnp.float32)
        tail_keys = key_blk * block_tail[:, None]
        next_state = jnp.dot(tail_keys.T, value_blk, precision=HIGHEST) + carry_keep * carry_state
        next_norm = lax.optimization_barrier(jnp.sum(tail_keys, axis=0)) + carry_keep * carry_norm
        return ((next_state, next_norm), numerator / denominator[:, None])
    stacked = (query_feat.reshape(pieces, span_len, -1), key_feat.reshape(pieces, span_len, -1), value_rows.reshape(pieces, span_len, -1), begins.reshape(pieces, span_len), (jnp.arange(pieces, dtype=jnp.int32) * span_len).astype(jnp.int32))
    initial = (jnp.zeros((query_feat.shape[1], value_rows.shape[1]), jnp.float32), jnp.zeros((query_feat.shape[1],), jnp.float32))
    swept_back = lax.scan(jax.checkpoint(advance), initial, stacked)
    return swept_back[1].reshape(total, value_rows.shape[1])

def reference(projected, out_grads, conv_weight, doc_lengths):
    total = projected.shape[0]
    positions = jnp.arange(total, dtype=jnp.int32)
    starts = (jnp.cumsum(doc_lengths) - doc_lengths).astype(jnp.int32)
    begins = lax.optimization_barrier(jnp.max(jnp.where(starts[None, :] <= positions[:, None], starts[None, :], 0), axis=1)).astype(jnp.int32)
    offsets = positions - begins
    keep_one = (offsets >= 1).astype(jnp.float32)[:, None]
    keep_two = (offsets >= 2).astype(jnp.float32)[:, None]
    head_width = 2 * KEY_DIM + HEAD_DIM
    scale_key = KEY_DIM ** (-0.25)

    def per_head(triple):
        return head_attention(triple, begins)

    def layer(signal, weights):
        mixed_rows = weights[0] * signal + weights[1] * shift_rows(signal, 1) * keep_one + weights[2] * shift_rows(signal, 2) * keep_two
        shaped = jnp.transpose(mixed_rows.reshape(total, HEADS, head_width), (1, 0, 2))
        queries = shaped[:, :, :KEY_DIM] * scale_key
        keys_all = shaped[:, :, KEY_DIM:2 * KEY_DIM] * scale_key
        values_all = shaped[:, :, 2 * KEY_DIM:]
        attended = lax.map(per_head, (queries, keys_all, values_all))
        return jnp.transpose(attended, (1, 0, 2)).reshape(total, HEADS * HEAD_DIM)
    primal, pullback = jax.vjp(layer, projected, conv_weight)
    results = pullback(out_grads)
    return (results[0], results[1])
```

```python
import functools
import math

import jax
import jax.numpy as jnp
from jax import lax
from jax.experimental import pallas as pl
from jax.experimental.pallas import tpu as pltpu
from jax.sharding import PartitionSpec as P

KEY_DIM = 16
HEAD_DIM = 128
HEADS = 16
WIDTH = 2 * KEY_DIM + HEAD_DIM
MEMBERS = 8
FEATS = 160
BLOCK = 256
LANES = 128
MESH = pl.DeviceIdType.MESH
F32 = jnp.float32
BF16 = jnp.bfloat16


def halves(x):
    high = x.astype(BF16)
    return high, (x - high.astype(F32)).astype(BF16)


def dot(a, b, ca=1, cb=0):
    return lax.dot_general(a, b, (((ca,), (cb,)), ((), ())), preferred_element_type=F32)


def dot_halves(a, b, ca=1, cb=0):
    return dot(a[0], b[0], ca, cb) + (dot(a[0], b[1], ca, cb) + dot(a[1], b[0], ca, cb))


def features(x):
    twice = jnp.concatenate([x, x], axis=0)
    parts = [x * x * (1.0 / math.sqrt(2.0))]
    for d in range(1, 8):
        parts.append(x * twice[d : d + 16])
    parts.append(x[0:8] * x[8:16])
    parts.append(x)
    row = lax.broadcasted_iota(jnp.int32, (8, x.shape[1]), 0)
    parts.append((row == 0).astype(F32))
    return jnp.concatenate(parts, axis=0)


def features_pull(x, grad):
    twice = jnp.concatenate([x, x], axis=0)
    total = math.sqrt(2.0) * x * grad[0:16] + grad[136:152]
    for d in range(1, 8):
        g = grad[16 * d : 16 * d + 16]
        back = g * x
        back = jnp.concatenate([back, back], axis=0)[16 - d : 32 - d]
        total = total + g * twice[d : d + 16] + back
    g = grad[128:136]
    return total + jnp.concatenate([g * x[8:16], g * x[0:8]], axis=0)


def kernel(
    sub, side, groups, seq_name, head_name,
    docs_ref, p_ref, o_ref, wv_ref, wqk_ref,
    gp_ref, gw_ref,
    sv, sqk, v_buf, qk_buf, o_buf,
    bcol, brow, vm, qkm, qrow, kst, qf, kf,
    num, den, gn_buf, gd_buf,
    s_buf, n_buf, g_buf, gd_state, n_row, s_sum,
    dmv, dmqk, dvt, rv, rqk, wmsg, wtot,
    in_send, in_recv, halo_sem, state_send, state_recv,
    back_halo, out_send, out_recv, w_send, w_recv, wt_send, wt_recv,
):
    members = sub * side
    hpd = HEADS // members
    rows = p_ref.shape[0]
    tokens = rows * members
    total_len = tokens * groups
    ndoc = docs_ref.shape[0]
    seq = lax.axis_index(seq_name)
    group = seq // sub
    me = (seq % sub) * side + lax.axis_index(head_name)
    base = group * tokens

    def device(g, m):
        return (g * sub + m // side, m % side)

    def remote(src, dst, send, recv, target):
        return pltpu.make_async_remote_copy(
            src_ref=src, dst_ref=dst, send_sem=send, recv_sem=recv, device_id=target, device_id_type=MESH
        )

    barrier = pltpu.get_barrier_semaphore()

    def greet_member(r, _):
        pl.semaphore_signal(barrier, inc=1, device_id=device(group, (me + r) % members), device_id_type=MESH)
        return 0

    def greet_group(r, _):
        pl.semaphore_signal(barrier, inc=1, device_id=device((group + r) % groups, me), device_id_type=MESH)
        return 0

    lax.fori_loop(1, members, greet_member, 0)
    lax.fori_loop(1, groups, greet_group, 0)

    for n in range(HEADS):
        d, h = n // hpd, n % hpd
        first = WIDTH * n
        tile = (first // LANES) * LANES
        off = first - tile
        turned = p_ref[:, tile : tile + LANES].T
        sqk[d, 32 * h : 32 * h + 32, :] = turned[off : off + 32, :]
        sv[d, :, HEAD_DIM * h : HEAD_DIM * h + HEAD_DIM] = p_ref[:, first + 32 : first + WIDTH]

    pl.semaphore_wait(barrier, members - 1 + groups - 1)

    def in_copies(m, slot, target):
        at = pl.ds(pl.multiple_of(rows * slot, rows), rows)
        at_v = pl.ds(pl.multiple_of(rows * slot + 8, 8), rows)
        lanes = pl.ds(pl.multiple_of(m * hpd * HEAD_DIM, LANES), hpd * HEAD_DIM)
        return (
            remote(sqk.at[m], qk_buf.at[slot + 1], in_send.at[0, m], in_recv.at[0, slot], target),
            remote(sv.at[m], v_buf.at[at_v, :], in_send.at[1, m], in_recv.at[1, slot], target),
            remote(o_ref.at[:, lanes], o_buf.at[at, :], in_send.at[2, m], in_recv.at[2, slot], target),
        )

    def send_some(picked):
        def body(r, _):
            m = (me + r) % members
            copies = in_copies(m, me, device(group, m))
            for k in picked:
                copies[k].start()
            return 0

        lax.fori_loop(1, members, body, 0)

    def wait_some(picked):
        def body(r, _):
            m = (me + members - r) % members
            copies = in_copies(m, m, device(group, m))
            for k in picked:
                copies[k].wait_recv()
            return 0

        lax.fori_loop(1, members, body, 0)

    send_some((0, 1))
    send_some((2,))
    qk_buf[me + 1] = sqk[me]
    v_buf[pl.ds(pl.multiple_of(rows * me + 8, 8), rows), :] = sv[me]
    o_buf[pl.ds(pl.multiple_of(rows * me, rows), rows), :] = o_ref[
        :, pl.ds(pl.multiple_of(me * hpd * HEAD_DIM, LANES), hpd * HEAD_DIM)
    ]

    starts = []
    run = jnp.int32(0)
    for i in range(ndoc):
        starts.append(run)
        run = run + docs_ref[i]

    def begin_of(pos):
        out = jnp.zeros_like(pos)
        for s in starts:
            out = jnp.where(s <= pos, s, out)
        return out

    bcol[...] = begin_of(base + lax.broadcasted_iota(jnp.int32, (tokens, LANES), 0))
    pos_row = base + lax.broadcasted_iota(jnp.int32, (8, tokens), 1)
    brow[...] = begin_of(pos_row)
    my_first = begin_of(base)
    my_last = begin_of(base + tokens - 1)

    wait_some((0, 1))
    nxt, prv = (group + 1) % groups, (group + groups - 1) % groups
    halo = (
        remote(qk_buf.at[members], qk_buf.at[0], halo_sem.at[0], halo_sem.at[1], device(nxt, me)),
        remote(v_buf.at[pl.ds(tokens, 8), :], v_buf.at[pl.ds(0, 8), :], halo_sem.at[2], halo_sem.at[3], device(nxt, me)),
    )
    for c in halo:
        c.start()
    for c in halo:
        c.wait()

    pos = pos_row[0:1]
    beg = brow[0:1, :]
    off_row = pos - beg
    m1_row = (off_row >= 1).astype(F32)
    m2_row = (off_row >= 2).astype(F32)
    lead_row = (beg < base).astype(F32)
    tail_row = (beg == my_last).astype(F32)
    w_cols = [wqk_ref[:, j : j + 1] for j in range(3)]

    def qk_signal():
        sig = jnp.concatenate([qk_buf[m] for m in range(members + 1)], axis=1)
        return sig[:, LANES:], pltpu.roll(sig, 1, 1)[:, LANES:], pltpu.roll(sig, 2, 1)[:, LANES:]

    s0, s1, s2 = qk_signal()
    qkm[...] = (w_cols[0] * s0 + w_cols[1] * (s1 * m1_row) + w_cols[2] * (s2 * m2_row)) * (KEY_DIM ** (-0.25))

    def col_masks(t0, count):
        pcol = base + t0 + lax.broadcasted_iota(jnp.int32, (count, 1), 0)
        off = pcol - bcol[t0 : t0 + count, 0:1]
        return (off >= 1).astype(F32), (off >= 2).astype(F32)

    for b in range(tokens // BLOCK):
        t0 = b * BLOCK
        m1, m2 = col_masks(t0, BLOCK)
        a0 = v_buf[t0 + 8 : t0 + 8 + BLOCK, :]
        a1 = v_buf[t0 + 7 : t0 + 7 + BLOCK, :]
        a2 = v_buf[t0 + 6 : t0 + 6 + BLOCK, :]
        vm[t0 : t0 + BLOCK, :] = wv_ref[0:1, :] * a0 + wv_ref[1:2, :] * (a1 * m1) + wv_ref[2:3, :] * (a2 * m2)

    def head_lanes(h):
        return pl.ds(pl.multiple_of(h * HEAD_DIM, LANES), HEAD_DIM)

    def q_of(h):
        return qkm[pl.ds(pl.multiple_of(32 * h, 8), 16), :]

    def k_of(h):
        return qkm[pl.ds(pl.multiple_of(32 * h + 16, 8), 16), :]

    def key_state(h, _):
        k = k_of(h)
        kh, kl = halves(k)
        kst[h] = jnp.concatenate([kh, kl, kh, kl], axis=0)
        feat = halves(features(k) * tail_row)
        kf[h, 0], kf[h, 1] = feat
        s_buf[group, h] = dot_halves(feat, halves(vm[:, head_lanes(h)]))
        ones = jnp.ones((8, tokens), BF16)
        norm = dot(ones, feat[0], 1, 1) + dot(ones, feat[1], 1, 1)
        n_buf[group, h] = jnp.concatenate([norm, jnp.zeros((8, 256 - FEATS), F32)], axis=1)
        return 0

    lax.fori_loop(0, hpd, key_state, 0)

    def state_copies(big, small, kind, slot, g):
        target = device(g, me)
        return (
            remote(big.at[slot], big.at[slot], state_send.at[kind, 0, g], state_recv.at[kind, 0, slot], target),
            remote(small.at[slot], small.at[slot], state_send.at[kind, 1, g], state_recv.at[kind, 1, slot], target),
        )

    def send_states(big, small, kind):
        def body(r, _):
            for c in state_copies(big, small, kind, group, (group + r) % groups):
                c.start()
            return 0

        lax.fori_loop(1, groups, body, 0)

    def wait_states(big, small, kind):
        def body(r, _):
            g = (group + groups - r) % groups
            for c in state_copies(big, small, kind, g, g):
                c.wait_recv()
            return 0

        lax.fori_loop(1, groups, body, 0)

    send_states(s_buf, n_buf, 0)

    def scores(h, i):
        wide = (i + 1) * BLOCK
        t0 = i * BLOCK
        u = 1.0 + dot(qrow[h, t0 : t0 + BLOCK, :], kst[h, :, 0:wide])
        s_pos = lax.broadcasted_iota(jnp.int32, (BLOCK, wide), 1)
        t_pos = t0 + lax.broadcasted_iota(jnp.int32, (BLOCK, wide), 0)
        begin = bcol[t0 : t0 + BLOCK, 0:1] - base
        allowed = (s_pos >= begin) & (s_pos <= t_pos)
        return allowed, u, jnp.where(allowed, 0.5 + 0.5 * (u * u), 0.0)

    def forward(h, _):
        q = q_of(h)
        qh, ql = halves(q)
        qh, ql = qh.astype(F32), ql.astype(F32)
        qrow[h] = jnp.concatenate([qh, qh, ql, ql], axis=0).T.astype(BF16)
        qf[h, 0], qf[h, 1] = halves(features(q) * lead_row)
        vh, vl = halves(vm[:, head_lanes(h)])
        both = jnp.concatenate([vh, vl], axis=1)
        for i in range(tokens // BLOCK):
            t0, wide = i * BLOCK, (i + 1) * BLOCK
            _, _, sc = scores(h, i)
            sh, sl = halves(sc)
            wide_num = dot(sh, both[0:wide])
            num[h, t0 : t0 + BLOCK, :] = wide_num[:, 0:128] + (wide_num[:, 128:256] + dot(sl, vh[0:wide]))
            den[h, t0 : t0 + BLOCK, :] = jnp.broadcast_to(jnp.sum(sc, axis=1, keepdims=True), (BLOCK, LANES))
        return 0

    lax.fori_loop(0, hpd, forward, 0)
    wait_some((2,))
    wait_states(s_buf, n_buf, 0)

    s_sum[...] = jnp.zeros_like(s_sum)
    n_row[...] = jnp.zeros_like(n_row)

    def add_earlier(g, _):
        last = begin_of(g * tokens + tokens - 1)
        weight = ((g < group) & (last == my_first)).astype(F32)
        s_sum[...] = s_sum[...] + weight * s_buf[g]
        n_row[...] = n_row[...] + weight * n_buf[g]
        return 0

    lax.fori_loop(0, groups, add_earlier, 0)

    def normalise(h, _):
        norm = jnp.broadcast_to(n_row[h, 0:1, 0:FEATS], (HEAD_DIM, FEATS))
        left = halves(jnp.concatenate([s_sum[h].T, norm], axis=0))
        for i in range(tokens // BLOCK):
            t0 = i * BLOCK
            carried = dot_halves(left, (qf[h, 0, :, t0 : t0 + BLOCK], qf[h, 1, :, t0 : t0 + BLOCK])).T
            n_all = num[h, t0 : t0 + BLOCK, :] + carried[:, 0:128]
            inv = 1.0 / (den[h, t0 : t0 + BLOCK, :] + carried[:, 128:256])
            gn = o_buf[t0 : t0 + BLOCK, head_lanes(h)] * inv
            gn_buf[h, t0 : t0 + BLOCK, :] = gn
            gd = -jnp.sum(gn * (n_all * inv), axis=1, keepdims=True)
            gd_buf[h, t0 : t0 + BLOCK, :] = jnp.broadcast_to(gd, (BLOCK, LANES))
        feat = (qf[h, 0], qf[h, 1])
        g_buf[group, h] = dot_halves(feat, halves(gn_buf[h]))
        gd_t = gd_buf[h].T[0:8]
        norm = dot_halves(halves(gd_t), feat, 1, 1)
        gd_state[group, h] = jnp.concatenate([norm, jnp.zeros((8, 256 - FEATS), F32)], axis=1)
        return 0

    lax.fori_loop(0, hpd, normalise, 0)
    send_states(g_buf, gd_state, 1)

    def column(row):
        return jnp.broadcast_to(row, (LANES, 256)).T[0:FEATS, 0:1]

    def backward(h, _):
        vh, vl = halves(vm[:, head_lanes(h)])
        v_twice = jnp.concatenate([vh, vh], axis=1)
        qh, ql = halves(q_of(h))
        kh, kl = halves(k_of(h))
        q_both = jnp.concatenate([qh, ql], axis=0)
        k_both = jnp.concatenate([kh, kl], axis=0)
        dvt[h] = jnp.zeros((HEAD_DIM, tokens), F32)
        at_q = pl.ds(pl.multiple_of(32 * h, 8), 16)
        at_k = pl.ds(pl.multiple_of(32 * h + 16, 8), 16)
        dmqk[at_k, 0:tokens] = jnp.zeros((16, tokens), F32)
        for i in range(tokens // BLOCK):
            t0, wide = i * BLOCK, (i + 1) * BLOCK
            allowed, u, sc = scores(h, i)
            gn = gn_buf[h, t0 : t0 + BLOCK, :]
            gh, gl = halves(gn)
            ds = dot(jnp.concatenate([gh, gl], axis=1), v_twice[0:wide], 1, 1) + dot(gh, vl[0:wide], 1, 1)
            dx = jnp.where(allowed, (ds + gd_buf[h, t0 : t0 + BLOCK, 0:1]) * u, 0.0)
            dh, dl = halves(dx)
            sh, sl = halves(sc)
            gth, gtl = halves(gn.T)
            dv = dot(jnp.concatenate([gth, gtl], axis=0), sh)
            dvt[h, :, 0:wide] += dv[0:128] + (dv[128:256] + dot(gth, sl))
            dk = dot(q_both[:, t0 : t0 + BLOCK], dh)
            dmqk[at_k, 0:wide] += dk[0:16] + (dk[16:32] + dot(qh[:, t0 : t0 + BLOCK], dl))
            dq = dot(k_both[:, 0:wide], dh, 1, 1)
            dmqk[at_q, t0 : t0 + BLOCK] = dq[0:16] + (dq[16:32] + dot(kh[:, 0:wide], dl, 1, 1))
        gd_row = gd_buf[h].T[0:1]
        dqf = dot_halves(halves(s_sum[h]), halves(gn_buf[h]), 1, 1) + column(n_row[h, 0:1, :]) * gd_row
        dmqk[at_q, 0:tokens] += features_pull(q_of(h), dqf * lead_row)
        return 0

    lax.fori_loop(0, hpd, backward, 0)
    wait_states(g_buf, gd_state, 1)

    s_sum[...] = jnp.zeros_like(s_sum)
    n_row[...] = jnp.zeros_like(n_row)

    def add_later(g, _):
        first = begin_of(g * tokens)
        weight = ((g > group) & (first == my_last)).astype(F32)
        s_sum[...] = s_sum[...] + weight * g_buf[g]
        n_row[...] = n_row[...] + weight * gd_state[g]
        return 0

    lax.fori_loop(0, groups, add_later, 0)

    def finish(h, _):
        at_k = pl.ds(pl.multiple_of(32 * h + 16, 8), 16)
        dkf = dot_halves(halves(s_sum[h]), halves(vm[:, head_lanes(h)]), 1, 1) + column(n_row[h, 0:1, :])
        dmqk[at_k, 0:tokens] += features_pull(k_of(h), dkf * tail_row)
        dv = dvt[h] + dot_halves(halves(s_sum[h].T), (kf[h, 0], kf[h, 1]))
        dmv[0:tokens, head_lanes(h)] = dv.T
        return 0

    lax.fori_loop(0, hpd, finish, 0)
    dmqk[:, 0:tokens] = dmqk[:, 0:tokens] * (KEY_DIM ** (-0.25))

    def drain_in(r, _):
        m = (me + r) % members
        for c in in_copies(m, me, device(group, m)):
            c.wait_send()
        return 0

    lax.fori_loop(1, members, drain_in, 0)

    late = (
        remote(dmqk.at[:, pl.ds(0, LANES)], dmqk.at[:, pl.ds(tokens, LANES)], back_halo.at[0], back_halo.at[1], device(prv, me)),
        remote(dmv.at[pl.ds(0, 8), :], dmv.at[pl.ds(tokens, 8), :], back_halo.at[2], back_halo.at[3], device(prv, me)),
    )
    for c in late:
        c.start()
    for c in late:
        c.wait()

    far = tokens + LANES
    pos_far = base + lax.broadcasted_iota(jnp.int32, (1, far), 1)
    inside = pos_far < total_len
    off_far = pos_far - begin_of(pos_far)
    dm = dmqk[...]
    dm1 = jnp.where(inside & (off_far >= 1), dm, 0.0)
    dm2 = jnp.where(inside & (off_far >= 2), dm, 0.0)
    back = (
        w_cols[0] * dm[:, 0:tokens]
        + w_cols[1] * pltpu.roll(dm1, far - 1, 1)[:, 0:tokens]
        + w_cols[2] * pltpu.roll(dm2, far - 2, 1)[:, 0:tokens]
    )
    for m in range(members):
        sqk[m] = back[:, m * rows : m * rows + rows]
    s0, s1, s2 = qk_signal()
    taps = [
        jnp.sum(dm[:, 0:tokens] * s0, axis=1, keepdims=True),
        jnp.sum(dm1[:, 0:tokens] * s1, axis=1, keepdims=True),
        jnp.sum(dm2[:, 0:tokens] * s2, axis=1, keepdims=True),
    ]
    lane = lax.broadcasted_iota(jnp.int32, (LANES, LANES), 1)
    square = jnp.zeros((LANES, LANES), F32)
    for j in range(3):
        tall = jnp.concatenate([taps[j], jnp.zeros((LANES - taps[j].shape[0], 1), F32)], axis=0)
        square = jnp.where(lane == j, tall, square)
    wmsg[group, :, hpd * HEAD_DIM :] = square.T[0:8]

    sums = [jnp.zeros((1, hpd * HEAD_DIM), F32) for _ in range(3)]
    for m in range(members):
        t0 = m * rows
        count = rows + 8
        pcol = base + t0 + lax.broadcasted_iota(jnp.int32, (count, 1), 0)
        off = pcol - begin_of(pcol)
        ok = pcol < total_len
        d0 = dmv[t0 : t0 + count, :]
        d1 = jnp.where(ok & (off >= 1), d0, 0.0)
        d2 = jnp.where(ok & (off >= 2), d0, 0.0)
        sv[m] = wv_ref[0:1, :] * d0[0:rows] + wv_ref[1:2, :] * d1[1 : rows + 1] + wv_ref[2:3, :] * d2[2 : rows + 2]
        a0 = v_buf[t0 + 8 : t0 + 8 + rows, :]
        a1 = v_buf[t0 + 7 : t0 + 7 + rows, :]
        a2 = v_buf[t0 + 6 : t0 + 6 + rows, :]
        for j, (d, a) in enumerate(((d0, a0), (d1, a1), (d2, a2))):
            sums[j] = sums[j] + jnp.sum(d[0:rows] * a, axis=0, keepdims=True)
    wmsg[group, :, 0 : hpd * HEAD_DIM] = jnp.concatenate(sums + [jnp.zeros((5, hpd * HEAD_DIM), F32)], axis=0)

    def w_copy(slot, g):
        return remote(wmsg.at[slot], wmsg.at[slot], w_send.at[g], w_recv.at[slot], device(g, me))

    def send_w(r, _):
        w_copy(group, (group + r) % groups).start()
        return 0

    lax.fori_loop(1, groups, send_w, 0)

    def out_copies(m, slot):
        target = device(group, m)
        return (
            remote(sqk.at[m], rqk.at[slot], out_send.at[0, m], out_recv.at[0, slot], target),
            remote(sv.at[m], rv.at[slot], out_send.at[1, m], out_recv.at[1, slot], target),
        )

    def send_out(r, _):
        for c in out_copies((me + r) % members, me):
            c.start()
        return 0

    lax.fori_loop(1, members, send_out, 0)
    rqk[me] = sqk[me]
    rv[me] = sv[me]

    def wait_w(r, _):
        g = (group + groups - r) % groups
        w_copy(g, g).wait_recv()
        return 0

    lax.fori_loop(1, groups, wait_w, 0)
    wtot[me] = lax.fori_loop(0, groups, lambda g, acc: acc + wmsg[g], jnp.zeros(wmsg.shape[1:], F32))

    def send_t(r, _):
        m = (me + r) % members
        remote(wtot.at[me], wtot.at[me], wt_send.at[m], wt_recv.at[me], device(group, m)).start()
        return 0

    lax.fori_loop(1, members, send_t, 0)

    def wait_out(r, _):
        m = (me + members - r) % members
        for c in out_copies(m, m):
            c.wait_recv()
        remote(wtot.at[m], wtot.at[m], wt_send.at[m], wt_recv.at[m], device(group, m)).wait_recv()
        return 0

    lax.fori_loop(1, members, wait_out, 0)

    for n in range(HEADS):
        d, h = n // hpd, n % hpd
        first = WIDTH * n
        tall = jnp.concatenate([rqk[d, 32 * h : 32 * h + 32, :], jnp.zeros((96, rows), F32)], axis=0)
        gp_ref[:, first : first + 32] = tall.T[:, 0:32]
        gp_ref[:, first + 32 : first + WIDTH] = rv[d, :, HEAD_DIM * h : HEAD_DIM * h + HEAD_DIM]
        gw_ref[:, first : first + 32] = wtot[d, 0:3, hpd * HEAD_DIM + 32 * h : hpd * HEAD_DIM + 32 * h + 32]
        gw_ref[:, first + 32 : first + WIDTH] = wtot[d, 0:3, HEAD_DIM * h : HEAD_DIM * h + HEAD_DIM]

    def drain_members(r, _):
        m = (me + r) % members
        for c in out_copies(m, me):
            c.wait_send()
        remote(wtot.at[me], wtot.at[me], wt_send.at[m], wt_recv.at[me], device(group, m)).wait_send()
        return 0

    lax.fori_loop(1, members, drain_members, 0)

    def drain_groups(r, _):
        g = (group + r) % groups
        for c in state_copies(s_buf, n_buf, 0, group, g) + state_copies(g_buf, gd_state, 1, group, g):
            c.wait_send()
        w_copy(group, g).wait_send()
        return 0

    lax.fori_loop(1, groups, drain_groups, 0)


def on_device(sub, side, groups, projected, out_grads, conv_weight, doc_lengths):
    members = sub * side
    hpd = HEADS // members
    rows = projected.shape[0]
    tokens = rows * members
    me = (lax.axis_index("seq") % sub) * side + lax.axis_index("head")
    mine = lax.dynamic_slice_in_dim(conv_weight, me * hpd * WIDTH, hpd * WIDTH, 1).reshape(3, hpd, WIDTH)
    wqk = mine[:, :, 0:32].reshape(3, hpd * 32).T
    wv = mine[:, :, 32:].reshape(3, hpd * HEAD_DIM)
    wide = hpd * HEAD_DIM
    vmem = pltpu.VMEM
    dma = pltpu.SemaphoreType.DMA
    scratch = [
        vmem((members, rows, wide), F32),
        vmem((members, hpd * 32, rows), F32),
        vmem((tokens + 8, wide), F32),
        vmem((members + 1, hpd * 32, rows), F32),
        vmem((tokens, wide), F32),
        vmem((tokens, LANES), jnp.int32),
        vmem((8, tokens), jnp.int32),
        vmem((tokens, wide), F32),
        vmem((hpd * 32, tokens), F32),
        vmem((hpd, tokens, 64), BF16),
        vmem((hpd, 64, tokens), BF16),
        vmem((hpd, 2, FEATS, tokens), BF16),
        vmem((hpd, 2, FEATS, tokens), BF16),
        vmem((hpd, tokens, LANES), F32),
        vmem((hpd, tokens, LANES), F32),
        vmem((hpd, tokens, LANES), F32),
        vmem((hpd, tokens, LANES), F32),
        vmem((groups, hpd, FEATS, HEAD_DIM), F32),
        vmem((groups, hpd, 8, 256), F32),
        vmem((groups, hpd, FEATS, HEAD_DIM), F32),
        vmem((groups, hpd, 8, 256), F32),
        vmem((hpd, 8, 256), F32),
        vmem((hpd, FEATS, HEAD_DIM), F32),
        vmem((tokens + 8, wide), F32),
        vmem((hpd * 32, tokens + LANES), F32),
        vmem((hpd, HEAD_DIM, tokens), F32),
        vmem((members, rows, wide), F32),
        vmem((members, hpd * 32, rows), F32),
        vmem((groups, 8, wide + LANES), F32),
        vmem((members, 8, wide + LANES), F32),
        dma((3, members)),
        dma((3, members)),
        dma((4,)),
        dma((2, 2, groups)),
        dma((2, 2, groups)),
        dma((4,)),
        dma((2, members)),
        dma((2, members)),
        dma((groups,)),
        dma((groups,)),
        dma((members,)),
        dma((members,)),
    ]
    spec = pl.BlockSpec(memory_space=pltpu.VMEM)
    return pl.pallas_call(
        functools.partial(kernel, sub, side, groups, "seq", "head"),
        out_shape=(
            jax.ShapeDtypeStruct(projected.shape, F32),
            jax.ShapeDtypeStruct(conv_weight.shape, F32),
        ),
        in_specs=[pl.BlockSpec(memory_space=pltpu.SMEM), spec, spec, spec, spec],
        out_specs=(spec, spec),
        scratch_shapes=scratch,
        compiler_params=pltpu.CompilerParams(
            collective_id=0, has_side_effects=True, vmem_limit_bytes=60 * 1024 * 1024
        ),
        name="layer_backward",
    )(doc_lengths, projected, out_grads, wv, wqk)


def solution(mesh):
    side = mesh.shape["head"]
    sub = max(1, MEMBERS // side)
    groups = mesh.shape["seq"] // sub
    return jax.shard_map(
        functools.partial(on_device, sub, side, groups),
        mesh=mesh,
        in_specs=(P(("seq", "head"), None), P(("seq", "head"), None), P(), P()),
        out_specs=(P(("seq", "head"), None), P()),
        check_vma=False,
    )
```

```python
import functools
import math

import jax
import jax.numpy as jnp
from jax import lax
from jax.experimental import pallas as pl
from jax.experimental.pallas import tpu as pltpu
from jax.sharding import PartitionSpec as P

KEY_DIM = 16
HEAD_DIM = 128
HEADS = 16
WIDTH = 2 * KEY_DIM + HEAD_DIM
MEMBERS = 8
FEATS = 160
BLOCK = 256
LANES = 128
MESH = pl.DeviceIdType.MESH
F32 = jnp.float32
BF16 = jnp.bfloat16


def halves(x):
    high = x.astype(BF16)
    return high, (x - high.astype(F32)).astype(BF16)


def dot(a, b, ca=1, cb=0):
    return lax.dot_general(a, b, (((ca,), (cb,)), ((), ())), preferred_element_type=F32)


def dot_halves(a, b, ca=1, cb=0):
    return dot(a[0], b[0], ca, cb) + (dot(a[0], b[1], ca, cb) + dot(a[1], b[0], ca, cb))


def features(x):
    twice = jnp.concatenate([x, x], axis=0)
    parts = [x * x * (1.0 / math.sqrt(2.0))]
    for d in range(1, 8):
        parts.append(x * twice[d : d + 16])
    parts.append(x[0:8] * x[8:16])
    parts.append(x)
    row = lax.broadcasted_iota(jnp.int32, (8, x.shape[1]), 0)
    parts.append((row == 0).astype(F32))
    return jnp.concatenate(parts, axis=0)


def features_pull(x, grad):
    twice = jnp.concatenate([x, x], axis=0)
    total = math.sqrt(2.0) * x * grad[0:16] + grad[136:152]
    for d in range(1, 8):
        g = grad[16 * d : 16 * d + 16]
        back = g * x
        back = jnp.concatenate([back, back], axis=0)[16 - d : 32 - d]
        total = total + g * twice[d : d + 16] + back
    g = grad[128:136]
    return total + jnp.concatenate([g * x[8:16], g * x[0:8]], axis=0)


def kernel(
    sub, side, groups, reach, seq_name, head_name,
    docs_ref, p_ref, o_ref, w_ref,
    gp_ref, gw_ref,
    sv, sqk, v_buf, qk_buf, o_buf, wv_all, wqk_all,
    bcol, brow, vm, qkm, qrow, kst, qf, kf,
    num, den, gn_buf, gd_buf,
    s_buf, n_buf, g_buf, gd_state, n_row, s_sum,
    dmv, dmqk, dvt, rv, rqk, wmsg, wtot,
    in_send, in_recv, halo_send, halo_recv, state_send, state_recv,
    back_send, back_recv, out_send, out_recv, w_send, w_recv, wt_send, wt_recv,
):
    members = sub * side
    hpd = HEADS // members
    rows = p_ref.shape[0]
    tokens = rows * members
    total_len = tokens * groups
    ndoc = docs_ref.shape[0]
    seq = lax.axis_index(seq_name)
    group = seq // sub
    me = (seq % sub) * side + lax.axis_index(head_name)
    base = group * tokens
    nxt, prv = (group + 1) % groups, (group + groups - 1) % groups
    is_last = me == members - 1

    def device(g, m):
        return (g * sub + m // side, m % side)

    def remote(src, dst, send, recv, target):
        return pltpu.make_async_remote_copy(
            src_ref=src, dst_ref=dst, send_sem=send, recv_sem=recv, device_id=target, device_id_type=MESH
        )

    def loop(low, high, body):
        def step(r, _):
            body(r)
            return 0

        lax.fori_loop(low, high, step, 0)

    barrier = pltpu.get_barrier_semaphore()

    def greet(target):
        pl.semaphore_signal(barrier, inc=1, device_id=target, device_id_type=MESH)

    loop(1, members, lambda r: greet(device(group, (me + r) % members)))
    loop(1, groups, lambda r: greet(device((group + r) % groups, me)))

    @pl.when(is_last)
    def _():
        loop(0, members - 1, lambda m: greet(device(nxt, m)))

    @pl.when(jnp.logical_not(is_last))
    def _():
        greet(device(prv, members - 1))

    for n in range(HEADS):
        d, h = n // hpd, n % hpd
        first = WIDTH * n
        tile = (first // LANES) * LANES
        off = first - tile
        turned = p_ref[:, tile : tile + LANES].T
        sqk[d, h] = turned[off : off + 32, :]
        sv[d, h] = p_ref[:, first + 32 : first + WIDTH]

    pl.semaphore_wait(barrier, members - 1 + groups - 1 + jnp.where(is_last, members - 1, 1))

    def qk_copy(h, m, slot):
        return remote(
            sqk.at[m, h], qk_buf.at[slot + 1, h], in_send.at[0, h, m], in_recv.at[0, h, slot], device(group, m)
        )

    def v_copy(h, m, slot):
        at = pl.ds(pl.multiple_of(rows * slot + 8, 8), rows)
        return remote(
            sv.at[m, h], v_buf.at[h, at, :], in_send.at[1, h, m], in_recv.at[1, h, slot], device(group, m)
        )

    def o_lanes(h, m):
        return pl.ds(pl.multiple_of((m * hpd + h) * HEAD_DIM, LANES), HEAD_DIM)

    def o_copy(h, m, slot):
        at = pl.ds(pl.multiple_of(rows * slot, rows), rows)
        return remote(
            o_ref.at[:, o_lanes(h, m)], o_buf.at[h, at, :], in_send.at[2, h, m], in_recv.at[2, h, slot],
            device(group, m),
        )

    def halo_qk(h, m, to):
        return remote(sqk.at[m, h], qk_buf.at[0, h], halo_send.at[0, h, m], halo_recv.at[0, h], device(to, m))

    def halo_v(h, m, to):
        return remote(
            sv.at[m, h, pl.ds(rows - 8, 8), :], v_buf.at[h, pl.ds(0, 8), :],
            halo_send.at[1, h, m], halo_recv.at[1, h], device(to, m),
        )

    def send_in(h):
        @pl.when(is_last)
        def _():
            def one(m):
                halo_qk(h, m, nxt).start()
                halo_v(h, m, nxt).start()

            loop(0, members, one)

        def one(r):
            m = (me + r) % members
            qk_copy(h, m, me).start()
            v_copy(h, m, me).start()

        loop(1, members, one)

    loop(0, hpd, send_in)
    loop(0, hpd, lambda h: loop(1, members, lambda r: o_copy(h, (me + r) % members, me).start()))

    def keep_own(h):
        qk_buf[me + 1, h] = sqk[me, h]
        v_buf[h, pl.ds(pl.multiple_of(rows * me + 8, 8), rows), :] = sv[me, h]
        o_buf[h, pl.ds(pl.multiple_of(rows * me, rows), rows), :] = o_ref[:, o_lanes(h, me)]

    loop(0, hpd, keep_own)

    for n in range(HEADS):
        d, h = n // hpd, n % hpd
        first = WIDTH * n
        tile = (first // LANES) * LANES
        off = first - tile
        square = jnp.concatenate([w_ref[:, tile : tile + LANES], jnp.zeros((LANES - 3, LANES), F32)], axis=0)
        wqk_all[d, h] = square.T[off : off + 32, :]
        wv_all[d, h, 0:3, :] = w_ref[:, first + 32 : first + WIDTH]

    starts = []
    run = jnp.int32(0)
    for i in range(ndoc):
        starts.append(run)
        run = run + docs_ref[i]

    def begin_of(pos):
        out = jnp.zeros_like(pos)
        for s in starts:
            out = jnp.where(s <= pos, s, out)
        return out

    bcol[...] = begin_of(base + lax.broadcasted_iota(jnp.int32, (tokens, LANES), 0))
    pos_row = base + lax.broadcasted_iota(jnp.int32, (8, tokens), 1)
    brow[...] = begin_of(pos_row)
    my_first = begin_of(base)
    my_last = begin_of(base + tokens - 1)

    pos = pos_row[0:1]
    beg = brow[0:1, :]
    off_row = pos - beg
    m1_row = (off_row >= 1).astype(F32)
    m2_row = (off_row >= 2).astype(F32)
    lead_row = (beg < base).astype(F32)
    tail_row = (beg == my_last).astype(F32)

    def qk_signal(h):
        sig = jnp.concatenate([qk_buf[m, h] for m in range(members + 1)], axis=1)
        return sig[:, LANES:], pltpu.roll(sig, 1, 1)[:, LANES:], pltpu.roll(sig, 2, 1)[:, LANES:]

    def taps_of(h):
        return [wqk_all[me, h, :, j : j + 1] for j in range(3)], [wv_all[me, h, j : j + 1, :] for j in range(3)]

    def q_of(h):
        return qkm[h, 0:16, :]

    def k_of(h):
        return qkm[h, 16:32, :]

    def state_copy(refs, kind, part, h, r):
        g = group + r if kind == 0 else group - r
        ref = refs[part]
        return remote(
            ref.at[0, h], ref.at[r, h], state_send.at[kind, part, h, r], state_recv.at[kind, part, h, r], device(g, me)
        )

    def ahead(kind, r):
        return group + r < groups if kind == 0 else group >= r

    def each_state(kind, to, body):
        def one(r):
            @pl.when(ahead(kind, r) if to else ahead(1 - kind, r))
            def _():
                body(r)

        loop(1, reach + 1, one)

    keys = (s_buf, n_buf)
    grads = (g_buf, gd_state)

    def arrive(h):
        def one(r):
            m = (me + members - r) % members
            qk_copy(h, m, m).wait_recv()
            v_copy(h, m, m).wait_recv()

        loop(1, members, one)
        halo_qk(h, me, prv).wait_recv()
        halo_v(h, me, prv).wait_recv()
        w_cols, w_rows = taps_of(h)
        s0, s1, s2 = qk_signal(h)
        qkm[h] = (w_cols[0] * s0 + w_cols[1] * (s1 * m1_row) + w_cols[2] * (s2 * m2_row)) * (KEY_DIM ** (-0.25))
        for b in range(tokens // BLOCK):
            t0 = b * BLOCK
            off = base + t0 + lax.broadcasted_iota(jnp.int32, (BLOCK, LANES), 0) - bcol[t0 : t0 + BLOCK, :]
            a0 = v_buf[h, t0 + 8 : t0 + 8 + BLOCK, :]
            a1 = jnp.where(off >= 1, v_buf[h, t0 + 7 : t0 + 7 + BLOCK, :], 0.0)
            a2 = jnp.where(off >= 2, v_buf[h, t0 + 6 : t0 + 6 + BLOCK, :], 0.0)
            vm[h, t0 : t0 + BLOCK, :] = w_rows[0] * a0 + w_rows[1] * a1 + w_rows[2] * a2
        k = k_of(h)
        kh, kl = halves(k)
        kst[h] = jnp.concatenate([kh, kl, kh, kl], axis=0)
        feat = halves(features(k) * tail_row)
        kf[h, 0], kf[h, 1] = feat
        ones = jnp.ones((8, tokens), BF16)
        norm = dot(ones, feat[0], 1, 1) + dot(ones, feat[1], 1, 1)
        n_buf[0, h] = jnp.concatenate([norm, jnp.zeros((8, 256 - FEATS), F32)], axis=1)
        each_state(0, True, lambda r: state_copy(keys, 0, 1, h, r).start())
        s_buf[0, h] = dot_halves(feat, halves(vm[h]))
        each_state(0, True, lambda r: state_copy(keys, 0, 0, h, r).start())

    loop(0, hpd, arrive)

    def scores(h, i):
        wide = (i + 1) * BLOCK
        t0 = i * BLOCK
        u = 1.0 + dot(qrow[h, t0 : t0 + BLOCK, :], kst[h, :, 0:wide])
        s_pos = lax.broadcasted_iota(jnp.int32, (BLOCK, wide), 1)
        t_pos = t0 + lax.broadcasted_iota(jnp.int32, (BLOCK, wide), 0)
        begin = bcol[t0 : t0 + BLOCK, 0:1] - base
        allowed = (s_pos >= begin) & (s_pos <= t_pos)
        return allowed, u, jnp.where(allowed, 0.5 + 0.5 * (u * u), 0.0)

    def forward(h):
        q = q_of(h)
        qh, ql = halves(q)
        qh, ql = qh.astype(F32), ql.astype(F32)
        qrow[h] = jnp.concatenate([qh, qh, ql, ql], axis=0).T.astype(BF16)
        qf[h, 0], qf[h, 1] = halves(features(q) * lead_row)
        vh, vl = halves(vm[h])
        both = jnp.concatenate([vh, vl], axis=1)
        for i in range(tokens // BLOCK):
            t0, wide = i * BLOCK, (i + 1) * BLOCK
            _, _, sc = scores(h, i)
            sh, sl = halves(sc)
            wide_num = dot(sh, both[0:wide])
            num[h, t0 : t0 + BLOCK, :] = wide_num[:, 0:128] + (wide_num[:, 128:256] + dot(sl, vh[0:wide]))
            den[h, t0 : t0 + BLOCK, :] = jnp.broadcast_to(jnp.sum(sc, axis=1, keepdims=True), (BLOCK, LANES))

    loop(0, hpd, forward)

    def gather(kind, part, refs, total, h):
        total[h] = jnp.zeros(total.shape[1:], F32)

        def add(r):
            if kind == 0:
                weight = begin_of((group - r) * tokens + tokens - 1) == my_first
            else:
                weight = begin_of((group + r) * tokens) == my_last
            state_copy(refs, kind, part, h, r).wait_recv()
            total[h] = total[h] + weight.astype(F32) * refs[part][r, h]

        each_state(kind, False, add)

    def normalise(h):
        loop(1, members, lambda r: o_copy(h, (me + members - r) % members, (me + members - r) % members).wait_recv())
        gather(0, 1, keys, n_row, h)
        feat = (qf[h, 0], qf[h, 1])
        norm = halves(jnp.broadcast_to(n_row[h, 0:1, 0:FEATS], (HEAD_DIM, FEATS)))
        for i in range(tokens // BLOCK):
            t0 = i * BLOCK
            carried = dot_halves(norm, (feat[0][:, t0 : t0 + BLOCK], feat[1][:, t0 : t0 + BLOCK])).T
            inv = 1.0 / (den[h, t0 : t0 + BLOCK, :] + carried)
            den[h, t0 : t0 + BLOCK, :] = inv
            gn_buf[h, t0 : t0 + BLOCK, :] = o_buf[h, t0 : t0 + BLOCK, :] * inv
        g_buf[0, h] = dot_halves(feat, halves(gn_buf[h]))
        each_state(1, True, lambda r: state_copy(grads, 1, 0, h, r).start())
        gather(0, 0, keys, s_sum, h)
        left = halves(s_sum[h].T)
        for i in range(tokens // BLOCK):
            t0 = i * BLOCK
            carried = dot_halves(left, (feat[0][:, t0 : t0 + BLOCK], feat[1][:, t0 : t0 + BLOCK])).T
            attended = (num[h, t0 : t0 + BLOCK, :] + carried) * den[h, t0 : t0 + BLOCK, :]
            gd = -jnp.sum(gn_buf[h, t0 : t0 + BLOCK, :] * attended, axis=1, keepdims=True)
            gd_buf[h, t0 : t0 + BLOCK, :] = jnp.broadcast_to(gd, (BLOCK, LANES))
        norm = dot_halves(halves(gd_buf[h].T[0:8]), feat, 1, 1)
        gd_state[0, h] = jnp.concatenate([norm, jnp.zeros((8, 256 - FEATS), F32)], axis=1)
        each_state(1, True, lambda r: state_copy(grads, 1, 1, h, r).start())

    loop(0, hpd, normalise)

    def column(row):
        return jnp.broadcast_to(row, (LANES, 256)).T[0:FEATS, 0:1]

    far = tokens + LANES
    pos_far = base + lax.broadcasted_iota(jnp.int32, (1, far), 1)
    off_far = jnp.where(pos_far < total_len, pos_far - begin_of(pos_far), 0)

    def back_qk(h):
        return remote(
            dmqk.at[h, :, pl.ds(0, LANES)], dmqk.at[h, :, pl.ds(tokens, LANES)],
            back_send.at[0, h], back_recv.at[0, h], device(prv, me),
        )

    def back_v(h):
        return remote(
            dmv.at[h, pl.ds(0, 8), :], dmv.at[h, pl.ds(tokens, 8), :],
            back_send.at[1, h], back_recv.at[1, h], device(prv, me),
        )

    def out_qk(h, m, slot):
        return remote(sqk.at[m, h], rqk.at[slot, h], out_send.at[0, h, m], out_recv.at[0, h, slot], device(group, m))

    def out_v(h, m, slot):
        return remote(sv.at[m, h], rv.at[slot, h], out_send.at[1, h, m], out_recv.at[1, h, slot], device(group, m))

    def backward(h):
        vh, vl = halves(vm[h])
        v_twice = jnp.concatenate([vh, vh], axis=1)
        qh, ql = halves(q_of(h))
        kh, kl = halves(k_of(h))
        q_both = jnp.concatenate([qh, ql], axis=0)
        k_both = jnp.concatenate([kh, kl], axis=0)
        dvt[h] = jnp.zeros((HEAD_DIM, tokens), F32)
        dmqk[h, 16:32, 0:tokens] = jnp.zeros((16, tokens), F32)
        for i in range(tokens // BLOCK):
            t0, wide = i * BLOCK, (i + 1) * BLOCK
            allowed, u, sc = scores(h, i)
            gn = gn_buf[h, t0 : t0 + BLOCK, :]
            gh, gl = halves(gn)
            ds = dot(jnp.concatenate([gh, gl], axis=1), v_twice[0:wide], 1, 1) + dot(gh, vl[0:wide], 1, 1)
            dx = jnp.where(allowed, (ds + gd_buf[h, t0 : t0 + BLOCK, 0:1]) * u, 0.0)
            dh, dl = halves(dx)
            sh, sl = halves(sc)
            gth, gtl = halves(gn.T)
            dv = dot(jnp.concatenate([gth, gtl], axis=0), sh)
            dvt[h, :, 0:wide] += dv[0:128] + (dv[128:256] + dot(gth, sl))
            dk = dot(q_both[:, t0 : t0 + BLOCK], dh)
            dmqk[h, 16:32, 0:wide] += dk[0:16] + (dk[16:32] + dot(qh[:, t0 : t0 + BLOCK], dl))
            dq = dot(k_both[:, 0:wide], dh, 1, 1)
            dmqk[h, 0:16, t0 : t0 + BLOCK] = dq[0:16] + (dq[16:32] + dot(kh[:, 0:wide], dl, 1, 1))
        gd_row = gd_buf[h].T[0:1]
        dqf = dot_halves(halves(s_sum[h]), halves(gn_buf[h]), 1, 1) + column(n_row[h, 0:1, :]) * gd_row
        dmqk[h, 0:16, 0:tokens] += features_pull(q_of(h), dqf * lead_row)

        gather(1, 0, grads, s_sum, h)
        dv = dvt[h] + dot_halves(halves(s_sum[h].T), (kf[h, 0], kf[h, 1]))
        dmv[h, 0:tokens, :] = dv.T
        back_v(h).start()
        gather(1, 1, grads, n_row, h)
        dkf = dot_halves(halves(s_sum[h]), halves(vm[h]), 1, 1) + column(n_row[h, 0:1, :])
        dmqk[h, 16:32, 0:tokens] += features_pull(k_of(h), dkf * tail_row)
        dmqk[h, :, 0:tokens] = dmqk[h, :, 0:tokens] * (KEY_DIM ** (-0.25))
        back_qk(h).start()

        def drain(r):
            m = (me + r) % members
            qk_copy(h, m, me).wait_send()
            v_copy(h, m, me).wait_send()

        loop(1, members, drain)

        @pl.when(is_last)
        def _():
            def one(m):
                halo_qk(h, m, nxt).wait_send()
                halo_v(h, m, nxt).wait_send()

            loop(0, members, one)

        w_cols, w_rows = taps_of(h)
        sums = [jnp.zeros((1, HEAD_DIM), F32) for _ in range(3)]
        for m in range(members):
            t0 = m * rows
            count = rows + 8
            if m == members - 1:
                back_v(h).wait()
            pcol = base + t0 + lax.broadcasted_iota(jnp.int32, (count, LANES), 0)
            off = jnp.where(pcol < total_len, pcol - begin_of(pcol), 0)
            d0 = dmv[h, t0 : t0 + count, :]
            d1 = jnp.where(off >= 1, d0, 0.0)
            d2 = jnp.where(off >= 2, d0, 0.0)
            sv[m, h] = w_rows[0] * d0[0:rows] + w_rows[1] * d1[1 : rows + 1] + w_rows[2] * d2[2 : rows + 2]
            for j, d in enumerate((d0, d1, d2)):
                past = v_buf[h, t0 + 8 - j : t0 + 8 - j + rows, :]
                sums[j] = sums[j] + jnp.sum(d[0:rows] * past, axis=0, keepdims=True)
        loop(1, members, lambda r: out_v(h, (me + r) % members, me).start())
        back_qk(h).wait()
        dm = dmqk[h]
        dm1 = jnp.where(off_far >= 1, dm, 0.0)
        dm2 = jnp.where(off_far >= 2, dm, 0.0)
        back = (
            w_cols[0] * dm[:, 0:tokens]
            + w_cols[1] * pltpu.roll(dm1, far - 1, 1)[:, 0:tokens]
            + w_cols[2] * pltpu.roll(dm2, far - 2, 1)[:, 0:tokens]
        )
        for m in range(members):
            sqk[m, h] = back[:, m * rows : m * rows + rows]
        loop(1, members, lambda r: out_qk(h, (me + r) % members, me).start())
        lane = lax.broadcasted_iota(jnp.int32, (LANES, LANES), 1)
        square = jnp.zeros((LANES, LANES), F32)
        for j, (d, sig) in enumerate(zip((dm, dm1, dm2), qk_signal(h))):
            tap = jnp.sum(d[:, 0:tokens] * sig, axis=1, keepdims=True)
            tall = jnp.concatenate([tap, jnp.zeros((LANES - 32, 1), F32)], axis=0)
            square = jnp.where(lane == j, tall, square)
        wmsg[group, h, :, LANES:] = square.T[0:8]
        wmsg[group, h, :, 0:LANES] = jnp.concatenate(sums + [jnp.zeros((5, HEAD_DIM), F32)], axis=0)
        rqk[me, h] = sqk[me, h]
        rv[me, h] = sv[me, h]

    loop(0, hpd, backward)

    def w_copy(slot, g):
        return remote(wmsg.at[slot], wmsg.at[slot], w_send.at[g], w_recv.at[slot], device(g, me))

    def t_copy(m, slot):
        return remote(wtot.at[slot], wtot.at[slot], wt_send.at[m], wt_recv.at[slot], device(group, m))

    loop(1, groups, lambda r: w_copy(group, (group + r) % groups).start())
    loop(1, groups, lambda r: w_copy((group + groups - r) % groups, (group + groups - r) % groups).wait_recv())
    wtot[me] = lax.fori_loop(0, groups, lambda g, acc: acc + wmsg[g], jnp.zeros(wmsg.shape[1:], F32))
    loop(1, members, lambda r: t_copy((me + r) % members, me).start())

    for h in range(hpd):
        def take(r):
            m = (me + members - r) % members
            out_v(h, m, m).wait_recv()
            out_qk(h, m, m).wait_recv()

        loop(1, members, take)
        for d in range(members):
            first = WIDTH * (d * hpd + h)
            tall = jnp.concatenate([rqk[d, h], jnp.zeros((96, rows), F32)], axis=0)
            gp_ref[:, first : first + 32] = tall.T[:, 0:32]
            gp_ref[:, first + 32 : first + WIDTH] = rv[d, h]

    def take_taps(r):
        m = (me + members - r) % members
        t_copy(m, m).wait_recv()

    loop(1, members, take_taps)
    for n in range(HEADS):
        d, h = n // hpd, n % hpd
        first = WIDTH * n
        gw_ref[:, first : first + 32] = wtot[d, h, 0:3, LANES : LANES + 32]
        gw_ref[:, first + 32 : first + WIDTH] = wtot[d, h, 0:3, 0:LANES]

    def drain_members(r):
        m = (me + r) % members

        def one(h):
            o_copy(h, m, me).wait_send()
            out_v(h, m, me).wait_send()
            out_qk(h, m, me).wait_send()

        loop(0, hpd, one)
        t_copy(m, me).wait_send()

    loop(1, members, drain_members)
    loop(1, groups, lambda r: w_copy(group, (group + r) % groups).wait_send())

    def drain_states(h):
        for kind, refs in enumerate((keys, grads)):
            for part in range(2):
                each_state(kind, True, lambda r: state_copy(refs, kind, part, h, r).wait_send())

    loop(0, hpd, drain_states)


def on_device(sub, side, groups, projected, out_grads, conv_weight, doc_lengths):
    members = sub * side
    hpd = HEADS // members
    rows = projected.shape[0]
    tokens = rows * members
    reach = max(1, groups // 2)
    vmem = pltpu.VMEM
    dma = pltpu.SemaphoreType.DMA
    scratch = [
        vmem((members, hpd, rows, HEAD_DIM), F32),
        vmem((members, hpd, 32, rows), F32),
        vmem((hpd, tokens + 8, HEAD_DIM), F32),
        vmem((members + 1, hpd, 32, rows), F32),
        vmem((hpd, tokens, HEAD_DIM), F32),
        vmem((members, hpd, 8, HEAD_DIM), F32),
        vmem((members, hpd, 32, LANES), F32),
        vmem((tokens, LANES), jnp.int32),
        vmem((8, tokens), jnp.int32),
        vmem((hpd, tokens, HEAD_DIM), F32),
        vmem((hpd, 32, tokens), F32),
        vmem((hpd, tokens, 64), BF16),
        vmem((hpd, 64, tokens), BF16),
        vmem((hpd, 2, FEATS, tokens), BF16),
        vmem((hpd, 2, FEATS, tokens), BF16),
        vmem((hpd, tokens, LANES), F32),
        vmem((hpd, tokens, LANES), F32),
        vmem((hpd, tokens, LANES), F32),
        vmem((hpd, tokens, LANES), F32),
        vmem((reach + 1, hpd, FEATS, HEAD_DIM), F32),
        vmem((reach + 1, hpd, 8, 256), F32),
        vmem((reach + 1, hpd, FEATS, HEAD_DIM), F32),
        vmem((reach + 1, hpd, 8, 256), F32),
        vmem((hpd, 8, 256), F32),
        vmem((hpd, FEATS, HEAD_DIM), F32),
        vmem((hpd, tokens + 8, HEAD_DIM), F32),
        vmem((hpd, 32, tokens + LANES), F32),
        vmem((hpd, HEAD_DIM, tokens), F32),
        vmem((members, hpd, rows, HEAD_DIM), F32),
        vmem((members, hpd, 32, rows), F32),
        vmem((groups, hpd, 8, 2 * LANES), F32),
        vmem((members, hpd, 8, 2 * LANES), F32),
        dma((3, hpd, members)),
        dma((3, hpd, members)),
        dma((2, hpd, members)),
        dma((2, hpd)),
        dma((2, 2, hpd, reach + 1)),
        dma((2, 2, hpd, reach + 1)),
        dma((2, hpd)),
        dma((2, hpd)),
        dma((2, hpd, members)),
        dma((2, hpd, members)),
        dma((groups,)),
        dma((groups,)),
        dma((members,)),
        dma((members,)),
    ]
    spec = pl.BlockSpec(memory_space=pltpu.VMEM)
    return pl.pallas_call(
        functools.partial(kernel, sub, side, groups, reach, "seq", "head"),
        out_shape=(
            jax.ShapeDtypeStruct(projected.shape, F32),
            jax.ShapeDtypeStruct(conv_weight.shape, F32),
        ),
        in_specs=[pl.BlockSpec(memory_space=pltpu.SMEM), spec, spec, spec],
        out_specs=(spec, spec),
        scratch_shapes=scratch,
        compiler_params=pltpu.CompilerParams(
            collective_id=0, has_side_effects=True, vmem_limit_bytes=60 * 1024 * 1024
        ),
        name="layer_backward",
    )(doc_lengths, projected, out_grads, conv_weight)


def solution(mesh):
    side = mesh.shape["head"]
    sub = max(1, MEMBERS // side)
    groups = mesh.shape["seq"] // sub
    return jax.shard_map(
        functools.partial(on_device, sub, side, groups),
        mesh=mesh,
        in_specs=(P(("seq", "head"), None), P(("seq", "head"), None), P(), P()),
        out_specs=(P(("seq", "head"), None), P()),
        check_vma=False,
    )
```

```python
import functools
import math

import jax
import jax.numpy as jnp
from jax import lax
from jax.experimental import pallas as pl
from jax.experimental.pallas import tpu as pltpu
from jax.sharding import PartitionSpec as P

KEY_DIM = 16
HEAD_DIM = 128
HEADS = 16
WIDTH = 2 * KEY_DIM + HEAD_DIM
MEMBERS = 8
FEATS = 160
BLOCK = 256
LANES = 128
MESH = pl.DeviceIdType.MESH
F32 = jnp.float32
BF16 = jnp.bfloat16


def halves(x):
    high = x.astype(BF16)
    return high, (x - high.astype(F32)).astype(BF16)


def dot(a, b, ca=1, cb=0):
    return lax.dot_general(a, b, (((ca,), (cb,)), ((), ())), preferred_element_type=F32)


def dot_halves(a, b, ca=1, cb=0):
    return dot(a[0], b[0], ca, cb) + (dot(a[0], b[1], ca, cb) + dot(a[1], b[0], ca, cb))


def features(x):
    twice = jnp.concatenate([x, x], axis=0)
    parts = [x * x * (1.0 / math.sqrt(2.0))]
    for d in range(1, 8):
        parts.append(x * twice[d : d + 16])
    parts.append(x[0:8] * x[8:16])
    parts.append(x)
    row = lax.broadcasted_iota(jnp.int32, (8, x.shape[1]), 0)
    parts.append((row == 0).astype(F32))
    return jnp.concatenate(parts, axis=0)


def features_pull(x, grad):
    twice = jnp.concatenate([x, x], axis=0)
    total = math.sqrt(2.0) * x * grad[0:16] + grad[136:152]
    for d in range(1, 8):
        g = grad[16 * d : 16 * d + 16]
        back = g * x
        back = jnp.concatenate([back, back], axis=0)[16 - d : 32 - d]
        total = total + g * twice[d : d + 16] + back
    g = grad[128:136]
    return total + jnp.concatenate([g * x[8:16], g * x[0:8]], axis=0)


def kernel(
    sub, side, groups, reach, seq_name, head_name,
    docs_ref, p_ref, o_ref, w_ref,
    rv, rqk, wt_ref,
    sv, sqk, v_buf, qk_buf, o_buf, wv_all, wqk_all,
    bcol, brow, vm, qkm, qrow, kst, qf, kf,
    num, den, gn_buf, gd_buf,
    s_buf, n_buf, g_buf, gd_state, n_row, s_sum,
    u_buf, sc_buf, dmv, dmqk, dvt, wmsg, wtot,
    in_send, in_recv, halo_send, halo_recv, state_send, state_recv,
    back_send, back_recv, out_send, out_recv, w_send, w_recv, wt_send, wt_recv, own_sem,
):
    members = sub * side
    hpd = HEADS // members
    rows = p_ref.shape[0]
    tokens = rows * members
    total_len = tokens * groups
    ndoc = docs_ref.shape[0]
    seq = lax.axis_index(seq_name)
    group = seq // sub
    me = (seq % sub) * side + lax.axis_index(head_name)
    base = group * tokens
    nxt, prv = (group + 1) % groups, (group + groups - 1) % groups
    is_last = me == members - 1

    def device(g, m):
        return (g * sub + m // side, m % side)

    def remote(src, dst, send, recv, target):
        return pltpu.make_async_remote_copy(
            src_ref=src, dst_ref=dst, send_sem=send, recv_sem=recv, device_id=target, device_id_type=MESH
        )

    def loop(low, high, body):
        def step(r, _):
            body(r)
            return 0

        lax.fori_loop(low, high, step, 0)

    barrier = pltpu.get_barrier_semaphore()

    def greet(target):
        pl.semaphore_signal(barrier, inc=1, device_id=target, device_id_type=MESH)

    loop(1, members, lambda r: greet(device(group, (me + r) % members)))
    loop(1, groups, lambda r: greet(device((group + r) % groups, me)))

    @pl.when(is_last)
    def _():
        loop(0, members - 1, lambda m: greet(device(nxt, m)))

    @pl.when(jnp.logical_not(is_last))
    def _():
        greet(device(prv, members - 1))

    def pack(h):
        for d in range(members):
            first = WIDTH * (d * hpd + h)
            tile = (first // LANES) * LANES
            off = first - tile
            turned = p_ref[:, tile : tile + LANES].T
            sqk[d, h] = turned[off : off + 32, :]
            sv[d, h] = p_ref[:, first + 32 : first + WIDTH]

    pack(0)
    pl.semaphore_wait(barrier, members - 1 + groups - 1 + jnp.where(is_last, members - 1, 1))

    def qk_copy(h, m, slot):
        return remote(
            sqk.at[m, h], qk_buf.at[slot + 1, h], in_send.at[0, h, m], in_recv.at[0, h, slot], device(group, m)
        )

    def v_copy(h, m, slot):
        at = pl.ds(pl.multiple_of(rows * slot + 8, 8), rows)
        return remote(
            sv.at[m, h], v_buf.at[h, at, :], in_send.at[1, h, m], in_recv.at[1, h, slot], device(group, m)
        )

    def o_lanes(h, m):
        return pl.ds(pl.multiple_of((m * hpd + h) * HEAD_DIM, LANES), HEAD_DIM)

    def o_copy(h, m, slot):
        at = pl.ds(pl.multiple_of(rows * slot, rows), rows)
        return remote(
            o_ref.at[:, o_lanes(h, m)], o_buf.at[h, at, :], in_send.at[2, h, m], in_recv.at[2, h, slot],
            device(group, m),
        )

    def halo_qk(h, m, to):
        return remote(sqk.at[m, h], qk_buf.at[0, h], halo_send.at[0, h, m], halo_recv.at[0, h], device(to, m))

    def halo_v(h, m, to):
        return remote(
            sv.at[m, h, pl.ds(rows - 8, 8), :], v_buf.at[h, pl.ds(0, 8), :],
            halo_send.at[1, h, m], halo_recv.at[1, h], device(to, m),
        )

    def send_in(h):
        @pl.when(is_last)
        def _():
            def one(m):
                halo_qk(h, m, nxt).start()
                halo_v(h, m, nxt).start()

            loop(0, members, one)

        def one(r):
            m = (me + r) % members
            qk_copy(h, m, me).start()
            v_copy(h, m, me).start()

        loop(1, members, one)

    send_in(0)
    for h in range(1, hpd):
        pack(h)
        send_in(h)
    loop(0, hpd, lambda h: loop(1, members, lambda r: o_copy(h, (me + r) % members, me).start()))

    def keep_own(h):
        qk_buf[me + 1, h] = sqk[me, h]
        v_buf[h, pl.ds(pl.multiple_of(rows * me + 8, 8), rows), :] = sv[me, h]
        o_buf[h, pl.ds(pl.multiple_of(rows * me, rows), rows), :] = o_ref[:, o_lanes(h, me)]

    loop(0, hpd, keep_own)

    for n in range(HEADS):
        d, h = n // hpd, n % hpd
        first = WIDTH * n
        tile = (first // LANES) * LANES
        off = first - tile
        square = jnp.concatenate([w_ref[:, tile : tile + LANES], jnp.zeros((LANES - 3, LANES), F32)], axis=0)
        wqk_all[d, h] = square.T[off : off + 32, :]
        wv_all[d, h, 0:3, :] = w_ref[:, first + 32 : first + WIDTH]

    starts = []
    run = jnp.int32(0)
    for i in range(ndoc):
        starts.append(run)
        run = run + docs_ref[i]

    def begin_of(pos):
        out = jnp.zeros_like(pos)
        for s in starts:
            out = jnp.where(s <= pos, s, out)
        return out

    bcol[...] = begin_of(base + lax.broadcasted_iota(jnp.int32, (tokens, LANES), 0))
    pos_row = base + lax.broadcasted_iota(jnp.int32, (8, tokens), 1)
    brow[...] = begin_of(pos_row)
    my_first = begin_of(base)
    my_last = begin_of(base + tokens - 1)

    pos = pos_row[0:1]
    beg = brow[0:1, :]
    off_row = pos - beg
    m1_row = (off_row >= 1).astype(F32)
    m2_row = (off_row >= 2).astype(F32)
    lead_row = (beg < base).astype(F32)
    tail_row = (beg == my_last).astype(F32)

    def qk_signal(h):
        sig = jnp.concatenate([qk_buf[m, h] for m in range(members + 1)], axis=1)
        return sig[:, LANES:], pltpu.roll(sig, 1, 1)[:, LANES:], pltpu.roll(sig, 2, 1)[:, LANES:]

    def taps_of(h):
        return [wqk_all[me, h, :, j : j + 1] for j in range(3)], [wv_all[me, h, j : j + 1, :] for j in range(3)]

    def q_of(h):
        return qkm[h, 0:16, :]

    def k_of(h):
        return qkm[h, 16:32, :]

    def state_copy(refs, kind, part, h, r):
        g = group + r if kind == 0 else group - r
        ref = refs[part]
        return remote(
            ref.at[0, h], ref.at[r, h], state_send.at[kind, part, h, r], state_recv.at[kind, part, h, r], device(g, me)
        )

    def ahead(kind, r):
        return group + r < groups if kind == 0 else group >= r

    def each_state(kind, to, body):
        def one(r):
            @pl.when(ahead(kind, r) if to else ahead(1 - kind, r))
            def _():
                body(r)

        loop(1, reach + 1, one)

    keys = (s_buf, n_buf)
    grads = (g_buf, gd_state)

    def arrive(h):
        def one(r):
            m = (me + members - r) % members
            qk_copy(h, m, m).wait_recv()
            v_copy(h, m, m).wait_recv()

        loop(1, members, one)
        halo_qk(h, me, prv).wait_recv()
        halo_v(h, me, prv).wait_recv()
        w_cols, w_rows = taps_of(h)
        s0, s1, s2 = qk_signal(h)
        qkm[h] = (w_cols[0] * s0 + w_cols[1] * (s1 * m1_row) + w_cols[2] * (s2 * m2_row)) * (KEY_DIM ** (-0.25))
        for b in range(tokens // BLOCK):
            t0 = b * BLOCK
            off = base + t0 + lax.broadcasted_iota(jnp.int32, (BLOCK, LANES), 0) - bcol[t0 : t0 + BLOCK, :]
            a0 = v_buf[h, t0 + 8 : t0 + 8 + BLOCK, :]
            a1 = jnp.where(off >= 1, v_buf[h, t0 + 7 : t0 + 7 + BLOCK, :], 0.0)
            a2 = jnp.where(off >= 2, v_buf[h, t0 + 6 : t0 + 6 + BLOCK, :], 0.0)
            vm[h, t0 : t0 + BLOCK, :] = w_rows[0] * a0 + w_rows[1] * a1 + w_rows[2] * a2
        k = k_of(h)
        kh, kl = halves(k)
        kst[h] = jnp.concatenate([kh, kl, kh, kl], axis=0)
        feat = halves(features(k) * tail_row)
        kf[h, 0], kf[h, 1] = feat
        ones = jnp.ones((8, tokens), BF16)
        norm = dot(ones, feat[0], 1, 1) + dot(ones, feat[1], 1, 1)
        n_buf[0, h] = jnp.concatenate([norm, jnp.zeros((8, 256 - FEATS), F32)], axis=1)
        each_state(0, True, lambda r: state_copy(keys, 0, 1, h, r).start())
        s_buf[0, h] = dot_halves(feat, halves(vm[h]))
        each_state(0, True, lambda r: state_copy(keys, 0, 0, h, r).start())

    def scores(h, i):
        wide = (i + 1) * BLOCK
        t0 = i * BLOCK
        u = 1.0 + dot(qrow[h, t0 : t0 + BLOCK, :], kst[h, :, 0:wide])
        s_pos = lax.broadcasted_iota(jnp.int32, (BLOCK, wide), 1)
        t_pos = t0 + lax.broadcasted_iota(jnp.int32, (BLOCK, wide), 0)
        begin = bcol[t0 : t0 + BLOCK, 0:1] - base
        allowed = (s_pos >= begin) & (s_pos <= t_pos)
        return jnp.where(allowed, u, 0.0), jnp.where(allowed, 0.5 + 0.5 * (u * u), 0.0)

    def forward(h):
        q = q_of(h)
        qh, ql = halves(q)
        qh, ql = qh.astype(F32), ql.astype(F32)
        qrow[h] = jnp.concatenate([qh, qh, ql, ql], axis=0).T.astype(BF16)
        qf[h, 0], qf[h, 1] = halves(features(q) * lead_row)
        vh, vl = halves(vm[h])
        both = jnp.concatenate([vh, vl], axis=1)
        for i in range(tokens // BLOCK):
            t0, wide = i * BLOCK, (i + 1) * BLOCK
            u, sc = scores(h, i)
            sh, sl = halves(sc)
            u_buf[h, t0 : t0 + BLOCK, 0:wide] = u
            sc_buf[h, 0, t0 : t0 + BLOCK, 0:wide] = sh
            sc_buf[h, 1, t0 : t0 + BLOCK, 0:wide] = sl
            wide_num = dot(sh, both[0:wide])
            num[h, t0 : t0 + BLOCK, :] = wide_num[:, 0:128] + (wide_num[:, 128:256] + dot(sl, vh[0:wide]))
            den[h, t0 : t0 + BLOCK, :] = jnp.broadcast_to(jnp.sum(sc, axis=1, keepdims=True), (BLOCK, LANES))

    def first_pass(h):
        arrive(h)
        forward(h)

    loop(0, hpd, first_pass)

    def gather(kind, part, refs, total, h):
        total[h] = jnp.zeros(total.shape[1:], F32)

        def add(r):
            if kind == 0:
                weight = begin_of((group - r) * tokens + tokens - 1) == my_first
            else:
                weight = begin_of((group + r) * tokens) == my_last
            state_copy(refs, kind, part, h, r).wait_recv()
            total[h] = total[h] + weight.astype(F32) * refs[part][r, h]

        each_state(kind, False, add)

    def normalise(h):
        loop(1, members, lambda r: o_copy(h, (me + members - r) % members, (me + members - r) % members).wait_recv())
        gather(0, 1, keys, n_row, h)
        feat = (qf[h, 0], qf[h, 1])
        norm = halves(jnp.broadcast_to(n_row[h, 0:1, 0:FEATS], (HEAD_DIM, FEATS)))
        for i in range(tokens // BLOCK):
            t0 = i * BLOCK
            carried = dot_halves(norm, (feat[0][:, t0 : t0 + BLOCK], feat[1][:, t0 : t0 + BLOCK])).T
            inv = 1.0 / (den[h, t0 : t0 + BLOCK, :] + carried)
            den[h, t0 : t0 + BLOCK, :] = inv
            gn_buf[h, t0 : t0 + BLOCK, :] = o_buf[h, t0 : t0 + BLOCK, :] * inv
        g_buf[0, h] = dot_halves(feat, halves(gn_buf[h]))
        each_state(1, True, lambda r: state_copy(grads, 1, 0, h, r).start())
        gather(0, 0, keys, s_sum, h)
        left = halves(s_sum[h].T)
        for i in range(tokens // BLOCK):
            t0 = i * BLOCK
            carried = dot_halves(left, (feat[0][:, t0 : t0 + BLOCK], feat[1][:, t0 : t0 + BLOCK])).T
            attended = (num[h, t0 : t0 + BLOCK, :] + carried) * den[h, t0 : t0 + BLOCK, :]
            gd = -jnp.sum(gn_buf[h, t0 : t0 + BLOCK, :] * attended, axis=1, keepdims=True)
            gd_buf[h, t0 : t0 + BLOCK, :] = jnp.broadcast_to(gd, (BLOCK, LANES))
        norm = dot_halves(halves(gd_buf[h].T[0:8]), feat, 1, 1)
        gd_state[0, h] = jnp.concatenate([norm, jnp.zeros((8, 256 - FEATS), F32)], axis=1)
        each_state(1, True, lambda r: state_copy(grads, 1, 1, h, r).start())

    loop(0, hpd, normalise)

    def column(row):
        return jnp.broadcast_to(row, (LANES, 256)).T[0:FEATS, 0:1]

    far = tokens + LANES
    pos_far = base + lax.broadcasted_iota(jnp.int32, (1, far), 1)
    off_far = jnp.where(pos_far < total_len, pos_far - begin_of(pos_far), 0)

    def back_qk(h):
        return remote(
            dmqk.at[h, :, pl.ds(0, LANES)], dmqk.at[h, :, pl.ds(tokens, LANES)],
            back_send.at[0, h], back_recv.at[0, h], device(prv, me),
        )

    def back_v(h):
        return remote(
            dmv.at[h, pl.ds(0, 8), :], dmv.at[h, pl.ds(tokens, 8), :],
            back_send.at[1, h], back_recv.at[1, h], device(prv, me),
        )

    def out_qk(h, m, slot):
        return remote(sqk.at[m, h], rqk.at[slot, h], out_send.at[0, h, m], out_recv.at[0, h, slot], device(group, m))

    def out_v(h, m, slot):
        return remote(sv.at[m, h], rv.at[slot, h], out_send.at[1, h, m], out_recv.at[1, h, slot], device(group, m))

    def own_copies(h):
        return (
            pltpu.make_async_copy(sv.at[me, h], rv.at[me, h], own_sem.at[0, h]),
            pltpu.make_async_copy(sqk.at[me, h], rqk.at[me, h], own_sem.at[1, h]),
        )

    def backward(h):
        vh, vl = halves(vm[h])
        v_twice = jnp.concatenate([vh, vh], axis=1)
        qh, ql = halves(q_of(h))
        kh, kl = halves(k_of(h))
        q_both = jnp.concatenate([qh, ql], axis=0)
        k_both = jnp.concatenate([kh, kl], axis=0)
        dvt[h] = jnp.zeros((HEAD_DIM, tokens), F32)
        dmqk[h, 16:32, 0:tokens] = jnp.zeros((16, tokens), F32)
        for i in range(tokens // BLOCK):
            t0, wide = i * BLOCK, (i + 1) * BLOCK
            gn = gn_buf[h, t0 : t0 + BLOCK, :]
            gh, gl = halves(gn)
            ds = dot(jnp.concatenate([gh, gl], axis=1), v_twice[0:wide], 1, 1) + dot(gh, vl[0:wide], 1, 1)
            dh, dl = halves((ds + gd_buf[h, t0 : t0 + BLOCK, 0:1]) * u_buf[h, t0 : t0 + BLOCK, 0:wide])
            sh, sl = sc_buf[h, 0, t0 : t0 + BLOCK, 0:wide], sc_buf[h, 1, t0 : t0 + BLOCK, 0:wide]
            gth, gtl = halves(gn.T)
            dv = dot(jnp.concatenate([gth, gtl], axis=0), sh)
            dvt[h, :, 0:wide] += dv[0:128] + (dv[128:256] + dot(gth, sl))
            dk = dot(q_both[:, t0 : t0 + BLOCK], dh)
            dmqk[h, 16:32, 0:wide] += dk[0:16] + (dk[16:32] + dot(qh[:, t0 : t0 + BLOCK], dl))
            dq = dot(k_both[:, 0:wide], dh, 1, 1)
            dmqk[h, 0:16, t0 : t0 + BLOCK] = dq[0:16] + (dq[16:32] + dot(kh[:, 0:wide], dl, 1, 1))
        gd_row = gd_buf[h].T[0:1]
        dqf = dot_halves(halves(s_sum[h]), halves(gn_buf[h]), 1, 1) + column(n_row[h, 0:1, :]) * gd_row
        dmqk[h, 0:16, 0:tokens] += features_pull(q_of(h), dqf * lead_row)

        gather(1, 0, grads, s_sum, h)
        dv = dvt[h] + dot_halves(halves(s_sum[h].T), (kf[h, 0], kf[h, 1]))
        dmv[h, 0:tokens, :] = dv.T
        back_v(h).start()
        gather(1, 1, grads, n_row, h)
        dkf = dot_halves(halves(s_sum[h]), halves(vm[h]), 1, 1) + column(n_row[h, 0:1, :])
        dmqk[h, 16:32, 0:tokens] += features_pull(k_of(h), dkf * tail_row)
        dmqk[h, :, 0:tokens] = dmqk[h, :, 0:tokens] * (KEY_DIM ** (-0.25))
        back_qk(h).start()

        def drain(r):
            m = (me + r) % members
            qk_copy(h, m, me).wait_send()
            v_copy(h, m, me).wait_send()

        loop(1, members, drain)

        @pl.when(is_last)
        def _():
            def one(m):
                halo_qk(h, m, nxt).wait_send()
                halo_v(h, m, nxt).wait_send()

            loop(0, members, one)

        w_cols, w_rows = taps_of(h)
        sums = [jnp.zeros((1, HEAD_DIM), F32) for _ in range(3)]
        for m in range(members):
            t0 = m * rows
            count = rows + 8
            if m == members - 1:
                back_v(h).wait()
            pcol = base + t0 + lax.broadcasted_iota(jnp.int32, (count, LANES), 0)
            off = jnp.where(pcol < total_len, pcol - begin_of(pcol), 0)
            d0 = dmv[h, t0 : t0 + count, :]
            d1 = jnp.where(off >= 1, d0, 0.0)
            d2 = jnp.where(off >= 2, d0, 0.0)
            sv[m, h] = w_rows[0] * d0[0:rows] + w_rows[1] * d1[1 : rows + 1] + w_rows[2] * d2[2 : rows + 2]
            for j, d in enumerate((d0, d1, d2)):
                past = v_buf[h, t0 + 8 - j : t0 + 8 - j + rows, :]
                sums[j] = sums[j] + jnp.sum(d[0:rows] * past, axis=0, keepdims=True)
        loop(1, members, lambda r: out_v(h, (me + r) % members, me).start())
        back_qk(h).wait()
        dm = dmqk[h]
        dm1 = jnp.where(off_far >= 1, dm, 0.0)
        dm2 = jnp.where(off_far >= 2, dm, 0.0)
        back = (
            w_cols[0] * dm[:, 0:tokens]
            + w_cols[1] * pltpu.roll(dm1, far - 1, 1)[:, 0:tokens]
            + w_cols[2] * pltpu.roll(dm2, far - 2, 1)[:, 0:tokens]
        )
        for m in range(members):
            sqk[m, h] = back[:, m * rows : m * rows + rows]
        loop(1, members, lambda r: out_qk(h, (me + r) % members, me).start())
        lane = lax.broadcasted_iota(jnp.int32, (LANES, LANES), 1)
        square = jnp.zeros((LANES, LANES), F32)
        for j, (d, sig) in enumerate(zip((dm, dm1, dm2), qk_signal(h))):
            tap = jnp.sum(d[:, 0:tokens] * sig, axis=1, keepdims=True)
            tall = jnp.concatenate([tap, jnp.zeros((LANES - 32, 1), F32)], axis=0)
            square = jnp.where(lane == j, tall, square)
        wmsg[group, h, :, LANES:] = square.T[0:8]
        wmsg[group, h, :, 0:LANES] = jnp.concatenate(sums + [jnp.zeros((5, HEAD_DIM), F32)], axis=0)
        for c in own_copies(h):
            c.start()

    loop(0, hpd, backward)

    def w_copy(slot, g):
        return remote(wmsg.at[slot], wmsg.at[slot], w_send.at[g], w_recv.at[slot], device(g, me))

    def t_copy(m, slot):
        return remote(wtot.at[slot], wtot.at[slot], wt_send.at[m], wt_recv.at[slot], device(group, m))

    loop(1, groups, lambda r: w_copy(group, (group + r) % groups).start())
    loop(1, groups, lambda r: w_copy((group + groups - r) % groups, (group + groups - r) % groups).wait_recv())
    wtot[me] = lax.fori_loop(0, groups, lambda g, acc: acc + wmsg[g], jnp.zeros(wmsg.shape[1:], F32))
    loop(1, members, lambda r: t_copy((me + r) % members, me).start())

    def take(h):
        def one(r):
            m = (me + members - r) % members
            out_v(h, m, m).wait_recv()
            out_qk(h, m, m).wait_recv()

        loop(1, members, one)
        for c in own_copies(h):
            c.wait()

    loop(0, hpd, take)

    def take_taps(r):
        m = (me + members - r) % members
        t_copy(m, m).wait_recv()

    loop(1, members, take_taps)
    wt_ref[...] = wtot[...]

    def drain_members(r):
        m = (me + r) % members

        def one(h):
            o_copy(h, m, me).wait_send()
            out_v(h, m, me).wait_send()
            out_qk(h, m, me).wait_send()

        loop(0, hpd, one)
        t_copy(m, me).wait_send()

    loop(1, members, drain_members)
    loop(1, groups, lambda r: w_copy(group, (group + r) % groups).wait_send())

    def drain_states(h):
        for kind, refs in enumerate((keys, grads)):
            for part in range(2):
                each_state(kind, True, lambda r: state_copy(refs, kind, part, h, r).wait_send())

    loop(0, hpd, drain_states)


def unpack(hpd, v_ref, qk_ref, taps_ref, gp_ref, gw_ref):
    rows = gp_ref.shape[0]
    for n in range(2 * hpd):
        d, h = n // hpd, n % hpd
        first = WIDTH * n
        tall = jnp.concatenate([qk_ref[d, h], jnp.zeros((LANES - 32, rows), F32)], axis=0)
        gp_ref[:, first : first + 32] = tall.T[:, 0:32]
        gp_ref[:, first + 32 : first + WIDTH] = v_ref[d, h]
        gw_ref[:, first : first + 32] = taps_ref[d, h, 0:3, LANES : LANES + 32]
        gw_ref[:, first + 32 : first + WIDTH] = taps_ref[d, h, 0:3, 0:LANES]


def on_device(sub, side, groups, projected, out_grads, conv_weight, doc_lengths):
    members = sub * side
    hpd = HEADS // members
    rows = projected.shape[0]
    tokens = rows * members
    reach = max(1, groups // 2)
    vmem = pltpu.VMEM
    dma = pltpu.SemaphoreType.DMA
    scratch = [
        vmem((members, hpd, rows, HEAD_DIM), F32),
        vmem((members, hpd, 32, rows), F32),
        vmem((hpd, tokens + 8, HEAD_DIM), F32),
        vmem((members + 1, hpd, 32, rows), F32),
        vmem((hpd, tokens, HEAD_DIM), F32),
        vmem((members, hpd, 8, HEAD_DIM), F32),
        vmem((members, hpd, 32, LANES), F32),
        vmem((tokens, LANES), jnp.int32),
        vmem((8, tokens), jnp.int32),
        vmem((hpd, tokens, HEAD_DIM), F32),
        vmem((hpd, 32, tokens), F32),
        vmem((hpd, tokens, 64), BF16),
        vmem((hpd, 64, tokens), BF16),
        vmem((hpd, 2, FEATS, tokens), BF16),
        vmem((hpd, 2, FEATS, tokens), BF16),
        vmem((hpd, tokens, LANES), F32),
        vmem((hpd, tokens, LANES), F32),
        vmem((hpd, tokens, LANES), F32),
        vmem((hpd, tokens, LANES), F32),
        vmem((reach + 1, hpd, FEATS, HEAD_DIM), F32),
        vmem((reach + 1, hpd, 8, 256), F32),
        vmem((reach + 1, hpd, FEATS, HEAD_DIM), F32),
        vmem((reach + 1, hpd, 8, 256), F32),
        vmem((hpd, 8, 256), F32),
        vmem((hpd, FEATS, HEAD_DIM), F32),
        vmem((hpd, tokens, tokens), F32),
        vmem((hpd, 2, tokens, tokens), BF16),
        vmem((hpd, tokens + 8, HEAD_DIM), F32),
        vmem((hpd, 32, tokens + LANES), F32),
        vmem((hpd, HEAD_DIM, tokens), F32),
        vmem((groups, hpd, 8, 2 * LANES), F32),
        vmem((members, hpd, 8, 2 * LANES), F32),
        dma((3, hpd, members)),
        dma((3, hpd, members)),
        dma((2, hpd, members)),
        dma((2, hpd)),
        dma((2, 2, hpd, reach + 1)),
        dma((2, 2, hpd, reach + 1)),
        dma((2, hpd)),
        dma((2, hpd)),
        dma((2, hpd, members)),
        dma((2, hpd, members)),
        dma((groups,)),
        dma((groups,)),
        dma((members,)),
        dma((members,)),
        dma((2, hpd)),
    ]
    spec = pl.BlockSpec(memory_space=pltpu.VMEM)
    returned = (members, hpd, rows, HEAD_DIM), (members, hpd, 32, rows), (members, hpd, 8, 2 * LANES)
    anywhere = pl.BlockSpec(memory_space=pl.ANY)
    values, columns, taps = pl.pallas_call(
        functools.partial(kernel, sub, side, groups, reach, "seq", "head"),
        out_shape=tuple(jax.ShapeDtypeStruct(shape, F32) for shape in returned),
        in_specs=[pl.BlockSpec(memory_space=pltpu.SMEM), spec, spec, spec],
        out_specs=(anywhere, anywhere, spec),
        scratch_shapes=scratch,
        compiler_params=pltpu.CompilerParams(
            collective_id=0, has_side_effects=True, vmem_limit_bytes=60 * 1024 * 1024
        ),
        name="layer_backward",
    )(doc_lengths, projected, out_grads, conv_weight)
    pair = 2 * hpd * WIDTH
    return pl.pallas_call(
        functools.partial(unpack, hpd),
        grid=(members // 2,),
        out_shape=(
            jax.ShapeDtypeStruct(projected.shape, F32),
            jax.ShapeDtypeStruct(conv_weight.shape, F32),
        ),
        in_specs=[
            pl.BlockSpec((2,) + shape[1:], lambda i: (i, 0, 0, 0)) for shape in returned
        ],
        out_specs=(pl.BlockSpec((rows, pair), lambda i: (0, i)), pl.BlockSpec((3, pair), lambda i: (0, i))),
        compiler_params=pltpu.CompilerParams(vmem_limit_bytes=60 * 1024 * 1024),
        name="unpack_heads",
    )(values, columns, taps)


def solution(mesh):
    side = mesh.shape["head"]
    sub = max(1, MEMBERS // side)
    groups = mesh.shape["seq"] // sub
    return jax.shard_map(
        functools.partial(on_device, sub, side, groups),
        mesh=mesh,
        in_specs=(P(("seq", "head"), None), P(("seq", "head"), None), P(), P()),
        out_specs=(P(("seq", "head"), None), P()),
        check_vma=False,
    )
```

```python
import functools
import math

import jax
import jax.numpy as jnp
from jax import lax
from jax.experimental import pallas as pl
from jax.experimental.pallas import tpu as pltpu
from jax.sharding import PartitionSpec as P

KEY_DIM = 16
HEAD_DIM = 128
HEADS = 16
WIDTH = 2 * KEY_DIM + HEAD_DIM
MEMBERS = 8
FEATS = 160
BLOCK = 256
LANES = 128
MESH = pl.DeviceIdType.MESH
F32 = jnp.float32
BF16 = jnp.bfloat16


def halves(x):
    high = x.astype(BF16)
    return high, (x - high.astype(F32)).astype(BF16)


def dot(a, b, ca=1, cb=0):
    return lax.dot_general(a, b, (((ca,), (cb,)), ((), ())), preferred_element_type=F32)


def dot_halves(a, b, ca=1, cb=0):
    return dot(a[0], b[0], ca, cb) + (dot(a[0], b[1], ca, cb) + dot(a[1], b[0], ca, cb))


def features(x):
    twice = jnp.concatenate([x, x], axis=0)
    parts = [x * x * (1.0 / math.sqrt(2.0))]
    for d in range(1, 8):
        parts.append(x * twice[d : d + 16])
    parts.append(x[0:8] * x[8:16])
    parts.append(x)
    row = lax.broadcasted_iota(jnp.int32, (8, x.shape[1]), 0)
    parts.append((row == 0).astype(F32))
    return jnp.concatenate(parts, axis=0)


def features_pull(x, grad):
    twice = jnp.concatenate([x, x], axis=0)
    total = math.sqrt(2.0) * x * grad[0:16] + grad[136:152]
    for d in range(1, 8):
        g = grad[16 * d : 16 * d + 16]
        back = g * x
        back = jnp.concatenate([back, back], axis=0)[16 - d : 32 - d]
        total = total + g * twice[d : d + 16] + back
    g = grad[128:136]
    return total + jnp.concatenate([g * x[8:16], g * x[0:8]], axis=0)


def kernel(
    sub, side, groups, reach, seq_name, head_name,
    docs_ref, p_ref, o_ref, w_ref,
    rv, rqk, wt_ref,
    sv, sqk, v_buf, qk_buf, o_buf, wv_all, wqk_all,
    bcol, brow, vm, qkm, qrow, kst, qf, kf,
    num, den, gn_buf, gd_buf,
    s_buf, n_buf, g_buf, gd_state, n_row, s_sum,
    u_buf, sc_buf, dmv, dmqk, dvt, wmsg, wtot,
    in_send, in_recv, halo_send, halo_recv, state_send, state_recv,
    back_send, back_recv, out_send, out_recv, w_send, w_recv, wt_send, wt_recv, own_sem,
):
    members = sub * side
    hpd = HEADS // members
    rows = p_ref.shape[0]
    tokens = rows * members
    total_len = tokens * groups
    ndoc = docs_ref.shape[0]
    seq = lax.axis_index(seq_name)
    group = seq // sub
    me = (seq % sub) * side + lax.axis_index(head_name)
    base = group * tokens
    nxt, prv = (group + 1) % groups, (group + groups - 1) % groups
    is_last = me == members - 1

    def device(g, m):
        return (g * sub + m // side, m % side)

    def remote(src, dst, send, recv, target):
        return pltpu.make_async_remote_copy(
            src_ref=src, dst_ref=dst, send_sem=send, recv_sem=recv, device_id=target, device_id_type=MESH
        )

    def loop(low, high, body):
        def step(r, _):
            body(r)
            return 0

        lax.fori_loop(low, high, step, 0)

    barrier = pltpu.get_barrier_semaphore()

    def greet(target):
        pl.semaphore_signal(barrier, inc=1, device_id=target, device_id_type=MESH)

    loop(1, members, lambda r: greet(device(group, (me + r) % members)))
    loop(1, groups, lambda r: greet(device((group + r) % groups, me)))

    @pl.when(is_last)
    def _():
        loop(0, members - 1, lambda m: greet(device(nxt, m)))

    @pl.when(jnp.logical_not(is_last))
    def _():
        greet(device(prv, members - 1))

    def pack(h):
        for d in range(members):
            first = WIDTH * (d * hpd + h)
            tile = (first // LANES) * LANES
            off = first - tile
            turned = p_ref[:, tile : tile + LANES].T
            sqk[d, h] = turned[off : off + 32, :]
            sv[d, h] = p_ref[:, first + 32 : first + WIDTH]

    pack(0)
    pl.semaphore_wait(barrier, members - 1 + groups - 1 + jnp.where(is_last, members - 1, 1))

    def qk_copy(h, m, slot):
        return remote(
            sqk.at[m, h], qk_buf.at[slot + 1, h], in_send.at[0, h, m], in_recv.at[0, h, slot], device(group, m)
        )

    def v_copy(h, m, slot):
        at = pl.ds(pl.multiple_of(rows * slot + 8, 8), rows)
        return remote(
            sv.at[m, h], v_buf.at[h, at, :], in_send.at[1, h, m], in_recv.at[1, h, slot], device(group, m)
        )

    def o_lanes(h, m):
        return pl.ds(pl.multiple_of((m * hpd + h) * HEAD_DIM, LANES), HEAD_DIM)

    def o_copy(h, m, slot):
        at = pl.ds(pl.multiple_of(rows * slot, rows), rows)
        return remote(
            o_ref.at[:, o_lanes(h, m)], o_buf.at[h, at, :], in_send.at[2, h, m], in_recv.at[2, h, slot],
            device(group, m),
        )

    def halo_qk(h, m, to):
        return remote(sqk.at[m, h], qk_buf.at[0, h], halo_send.at[0, h, m], halo_recv.at[0, h], device(to, m))

    def halo_v(h, m, to):
        return remote(
            sv.at[m, h, pl.ds(rows - 8, 8), :], v_buf.at[h, pl.ds(0, 8), :],
            halo_send.at[1, h, m], halo_recv.at[1, h], device(to, m),
        )

    def send_in(h):
        @pl.when(is_last)
        def _():
            def one(m):
                halo_qk(h, m, nxt).start()
                halo_v(h, m, nxt).start()

            loop(0, members, one)

        def one(r):
            m = (me + r) % members
            qk_copy(h, m, me).start()
            v_copy(h, m, me).start()

        loop(1, members, one)
        loop(1, members, lambda r: o_copy(h, (me + r) % members, me).start())

    send_in(0)
    for h in range(1, hpd):
        pack(h)
        send_in(h)

    def keep_own(h):
        qk_buf[me + 1, h] = sqk[me, h]
        v_buf[h, pl.ds(pl.multiple_of(rows * me + 8, 8), rows), :] = sv[me, h]
        o_buf[h, pl.ds(pl.multiple_of(rows * me, rows), rows), :] = o_ref[:, o_lanes(h, me)]

    loop(0, hpd, keep_own)

    for n in range(HEADS):
        d, h = n // hpd, n % hpd
        first = WIDTH * n
        tile = (first // LANES) * LANES
        off = first - tile
        square = jnp.concatenate([w_ref[:, tile : tile + LANES], jnp.zeros((LANES - 3, LANES), F32)], axis=0)
        wqk_all[d, h] = square.T[off : off + 32, :]
        wv_all[d, h, 0:3, :] = w_ref[:, first + 32 : first + WIDTH]

    starts = []
    run = jnp.int32(0)
    for i in range(ndoc):
        starts.append(run)
        run = run + docs_ref[i]

    def begin_of(pos):
        out = jnp.zeros_like(pos)
        for s in starts:
            out = jnp.where(s <= pos, s, out)
        return out

    bcol[...] = begin_of(base + lax.broadcasted_iota(jnp.int32, (tokens, LANES), 0))
    pos_row = base + lax.broadcasted_iota(jnp.int32, (8, tokens), 1)
    brow[...] = begin_of(pos_row)
    my_first = begin_of(base)
    my_last = begin_of(base + tokens - 1)

    pos = pos_row[0:1]
    beg = brow[0:1, :]
    off_row = pos - beg
    m1_row = (off_row >= 1).astype(F32)
    m2_row = (off_row >= 2).astype(F32)
    lead_row = (beg < base).astype(F32)
    tail_row = (beg == my_last).astype(F32)

    def qk_signal(h):
        sig = jnp.concatenate([qk_buf[m, h] for m in range(members + 1)], axis=1)
        return sig[:, LANES:], pltpu.roll(sig, 1, 1)[:, LANES:], pltpu.roll(sig, 2, 1)[:, LANES:]

    def taps_of(h):
        return [wqk_all[me, h, :, j : j + 1] for j in range(3)], [wv_all[me, h, j : j + 1, :] for j in range(3)]

    def q_of(h):
        return qkm[h, 0:16, :]

    def k_of(h):
        return qkm[h, 16:32, :]

    def state_copy(refs, kind, part, h, r):
        g = group + r if kind == 0 else group - r
        ref = refs[part]
        return remote(
            ref.at[0, h], ref.at[r, h], state_send.at[kind, part, h, r], state_recv.at[kind, part, h, r], device(g, me)
        )

    def ahead(kind, r):
        return group + r < groups if kind == 0 else group >= r

    def each_state(kind, to, body):
        def one(r):
            @pl.when(ahead(kind, r) if to else ahead(1 - kind, r))
            def _():
                body(r)

        loop(1, reach + 1, one)

    keys = (s_buf, n_buf)
    grads = (g_buf, gd_state)

    def arrive(h):
        def one(r):
            m = (me + members - r) % members
            qk_copy(h, m, m).wait_recv()
            v_copy(h, m, m).wait_recv()

        loop(1, members, one)
        halo_qk(h, me, prv).wait_recv()
        halo_v(h, me, prv).wait_recv()
        w_cols, w_rows = taps_of(h)
        s0, s1, s2 = qk_signal(h)
        qkm[h] = (w_cols[0] * s0 + w_cols[1] * (s1 * m1_row) + w_cols[2] * (s2 * m2_row)) * (KEY_DIM ** (-0.25))
        for b in range(tokens // BLOCK):
            t0 = b * BLOCK
            off = base + t0 + lax.broadcasted_iota(jnp.int32, (BLOCK, LANES), 0) - bcol[t0 : t0 + BLOCK, :]
            a0 = v_buf[h, t0 + 8 : t0 + 8 + BLOCK, :]
            a1 = jnp.where(off >= 1, v_buf[h, t0 + 7 : t0 + 7 + BLOCK, :], 0.0)
            a2 = jnp.where(off >= 2, v_buf[h, t0 + 6 : t0 + 6 + BLOCK, :], 0.0)
            vm[h, t0 : t0 + BLOCK, :] = w_rows[0] * a0 + w_rows[1] * a1 + w_rows[2] * a2
        k = k_of(h)
        kh, kl = halves(k)
        kst[h] = jnp.concatenate([kh, kl, kh, kl], axis=0)
        feat = halves(features(k) * tail_row)
        kf[h, 0], kf[h, 1] = feat
        ones = jnp.ones((8, tokens), BF16)
        norm = dot(ones, feat[0], 1, 1) + dot(ones, feat[1], 1, 1)
        n_buf[0, h] = jnp.concatenate([norm, jnp.zeros((8, 256 - FEATS), F32)], axis=1)
        each_state(0, True, lambda r: state_copy(keys, 0, 1, h, r).start())
        s_buf[0, h] = dot_halves(feat, halves(vm[h]))
        each_state(0, True, lambda r: state_copy(keys, 0, 0, h, r).start())

    def scores(h, i):
        wide = (i + 1) * BLOCK
        t0 = i * BLOCK
        u = 1.0 + dot(qrow[h, t0 : t0 + BLOCK, :], kst[h, :, 0:wide])
        s_pos = lax.broadcasted_iota(jnp.int32, (BLOCK, wide), 1)
        t_pos = t0 + lax.broadcasted_iota(jnp.int32, (BLOCK, wide), 0)
        begin = bcol[t0 : t0 + BLOCK, 0:1] - base
        allowed = (s_pos >= begin) & (s_pos <= t_pos)
        return jnp.where(allowed, u, 0.0), jnp.where(allowed, 0.5 + 0.5 * (u * u), 0.0)

    def forward(h):
        q = q_of(h)
        qh, ql = halves(q)
        qh, ql = qh.astype(F32), ql.astype(F32)
        qrow[h] = jnp.concatenate([qh, qh, ql, ql], axis=0).T.astype(BF16)
        qf[h, 0], qf[h, 1] = halves(features(q) * lead_row)
        vh, vl = halves(vm[h])
        both = jnp.concatenate([vh, vl], axis=1)
        for i in range(tokens // BLOCK):
            t0, wide = i * BLOCK, (i + 1) * BLOCK
            u, sc = scores(h, i)
            sh, sl = halves(sc)
            u_buf[h, t0 : t0 + BLOCK, 0:wide] = u
            sc_buf[h, 0, t0 : t0 + BLOCK, 0:wide] = sh
            sc_buf[h, 1, t0 : t0 + BLOCK, 0:wide] = sl
            wide_num = dot(sh, both[0:wide])
            num[h, t0 : t0 + BLOCK, :] = wide_num[:, 0:128] + (wide_num[:, 128:256] + dot(sl, vh[0:wide]))
            den[h, t0 : t0 + BLOCK, :] = jnp.broadcast_to(jnp.sum(sc, axis=1, keepdims=True), (BLOCK, LANES))

    def gather(kind, part, refs, total, h):
        total[h] = jnp.zeros(total.shape[1:], F32)

        def add(r):
            if kind == 0:
                weight = begin_of((group - r) * tokens + tokens - 1) == my_first
            else:
                weight = begin_of((group + r) * tokens) == my_last
            state_copy(refs, kind, part, h, r).wait_recv()
            total[h] = total[h] + weight.astype(F32) * refs[part][r, h]

        each_state(kind, False, add)

    def normalise(h):
        loop(1, members, lambda r: o_copy(h, (me + members - r) % members, (me + members - r) % members).wait_recv())
        gather(0, 1, keys, n_row, h)
        feat = (qf[h, 0], qf[h, 1])
        norm = halves(jnp.broadcast_to(n_row[h, 0:1, 0:FEATS], (HEAD_DIM, FEATS)))
        for i in range(tokens // BLOCK):
            t0 = i * BLOCK
            carried = dot_halves(norm, (feat[0][:, t0 : t0 + BLOCK], feat[1][:, t0 : t0 + BLOCK])).T
            inv = 1.0 / (den[h, t0 : t0 + BLOCK, :] + carried)
            den[h, t0 : t0 + BLOCK, :] = inv
            gn_buf[h, t0 : t0 + BLOCK, :] = o_buf[h, t0 : t0 + BLOCK, :] * inv
        g_buf[0, h] = dot_halves(feat, halves(gn_buf[h]))
        each_state(1, True, lambda r: state_copy(grads, 1, 0, h, r).start())
        gather(0, 0, keys, s_sum, h)
        left = halves(s_sum[h].T)
        for i in range(tokens // BLOCK):
            t0 = i * BLOCK
            carried = dot_halves(left, (feat[0][:, t0 : t0 + BLOCK], feat[1][:, t0 : t0 + BLOCK])).T
            attended = (num[h, t0 : t0 + BLOCK, :] + carried) * den[h, t0 : t0 + BLOCK, :]
            gd = -jnp.sum(gn_buf[h, t0 : t0 + BLOCK, :] * attended, axis=1, keepdims=True)
            gd_buf[h, t0 : t0 + BLOCK, :] = jnp.broadcast_to(gd, (BLOCK, LANES))
        norm = dot_halves(halves(gd_buf[h].T[0:8]), feat, 1, 1)
        gd_state[0, h] = jnp.concatenate([norm, jnp.zeros((8, 256 - FEATS), F32)], axis=1)
        each_state(1, True, lambda r: state_copy(grads, 1, 1, h, r).start())

    def column(row):
        return jnp.broadcast_to(row, (LANES, 256)).T[0:FEATS, 0:1]

    far = tokens + LANES
    pos_far = base + lax.broadcasted_iota(jnp.int32, (1, far), 1)
    off_far = jnp.where(pos_far < total_len, pos_far - begin_of(pos_far), 0)

    def back_qk(h):
        return remote(
            dmqk.at[h, :, pl.ds(0, LANES)], dmqk.at[h, :, pl.ds(tokens, LANES)],
            back_send.at[0, h], back_recv.at[0, h], device(prv, me),
        )

    def back_v(h):
        return remote(
            dmv.at[h, pl.ds(0, 8), :], dmv.at[h, pl.ds(tokens, 8), :],
            back_send.at[1, h], back_recv.at[1, h], device(prv, me),
        )

    def out_qk(h, m, slot):
        return remote(sqk.at[m, h], rqk.at[slot, h], out_send.at[0, h, m], out_recv.at[0, h, slot], device(group, m))

    def out_v(h, m, slot):
        return remote(sv.at[m, h], rv.at[slot, h], out_send.at[1, h, m], out_recv.at[1, h, slot], device(group, m))

    def own_copies(h):
        return (
            pltpu.make_async_copy(sv.at[me, h], rv.at[me, h], own_sem.at[0, h]),
            pltpu.make_async_copy(sqk.at[me, h], rqk.at[me, h], own_sem.at[1, h]),
        )

    def backward(h):
        vh, vl = halves(vm[h])
        v_twice = jnp.concatenate([vh, vh], axis=1)
        qh, ql = halves(q_of(h))
        kh, kl = halves(k_of(h))
        q_both = jnp.concatenate([qh, ql], axis=0)
        k_both = jnp.concatenate([kh, kl], axis=0)
        dvt[h] = jnp.zeros((HEAD_DIM, tokens), F32)
        dmqk[h, 16:32, 0:tokens] = jnp.zeros((16, tokens), F32)
        for i in range(tokens // BLOCK):
            t0, wide = i * BLOCK, (i + 1) * BLOCK
            gn = gn_buf[h, t0 : t0 + BLOCK, :]
            gh, gl = halves(gn)
            ds = dot(jnp.concatenate([gh, gl], axis=1), v_twice[0:wide], 1, 1) + dot(gh, vl[0:wide], 1, 1)
            dh, dl = halves((ds + gd_buf[h, t0 : t0 + BLOCK, 0:1]) * u_buf[h, t0 : t0 + BLOCK, 0:wide])
            sh, sl = sc_buf[h, 0, t0 : t0 + BLOCK, 0:wide], sc_buf[h, 1, t0 : t0 + BLOCK, 0:wide]
            gth, gtl = halves(gn.T)
            dv = dot(jnp.concatenate([gth, gtl], axis=0), sh)
            dvt[h, :, 0:wide] += dv[0:128] + (dv[128:256] + dot(gth, sl))
            dk = dot(q_both[:, t0 : t0 + BLOCK], dh)
            dmqk[h, 16:32, 0:wide] += dk[0:16] + (dk[16:32] + dot(qh[:, t0 : t0 + BLOCK], dl))
            dq = dot(k_both[:, 0:wide], dh, 1, 1)
            dmqk[h, 0:16, t0 : t0 + BLOCK] = dq[0:16] + (dq[16:32] + dot(kh[:, 0:wide], dl, 1, 1))
        gd_row = gd_buf[h].T[0:1]
        dqf = dot_halves(halves(s_sum[h]), halves(gn_buf[h]), 1, 1) + column(n_row[h, 0:1, :]) * gd_row
        dmqk[h, 0:16, 0:tokens] += features_pull(q_of(h), dqf * lead_row)

    def finish(h):
        gather(1, 0, grads, s_sum, h)
        dv = dvt[h] + dot_halves(halves(s_sum[h].T), (kf[h, 0], kf[h, 1]))
        dmv[h, 0:tokens, :] = dv.T
        back_v(h).start()
        gather(1, 1, grads, n_row, h)
        dkf = dot_halves(halves(s_sum[h]), halves(vm[h]), 1, 1) + column(n_row[h, 0:1, :])
        dmqk[h, 16:32, 0:tokens] += features_pull(k_of(h), dkf * tail_row)
        dmqk[h, :, 0:tokens] = dmqk[h, :, 0:tokens] * (KEY_DIM ** (-0.25))
        back_qk(h).start()

        def drain(r):
            m = (me + r) % members
            qk_copy(h, m, me).wait_send()
            v_copy(h, m, me).wait_send()

        loop(1, members, drain)

        @pl.when(is_last)
        def _():
            def one(m):
                halo_qk(h, m, nxt).wait_send()
                halo_v(h, m, nxt).wait_send()

            loop(0, members, one)

        w_cols, w_rows = taps_of(h)
        sums = [jnp.zeros((1, HEAD_DIM), F32) for _ in range(3)]
        for m in range(members):
            t0 = m * rows
            count = rows + 8
            if m == members - 1:
                back_v(h).wait()
            pcol = base + t0 + lax.broadcasted_iota(jnp.int32, (count, LANES), 0)
            off = jnp.where(pcol < total_len, pcol - begin_of(pcol), 0)
            d0 = dmv[h, t0 : t0 + count, :]
            d1 = jnp.where(off >= 1, d0, 0.0)
            d2 = jnp.where(off >= 2, d0, 0.0)
            sv[m, h] = w_rows[0] * d0[0:rows] + w_rows[1] * d1[1 : rows + 1] + w_rows[2] * d2[2 : rows + 2]
            for j, d in enumerate((d0, d1, d2)):
                past = v_buf[h, t0 + 8 - j : t0 + 8 - j + rows, :]
                sums[j] = sums[j] + jnp.sum(d[0:rows] * past, axis=0, keepdims=True)
        loop(1, members, lambda r: out_v(h, (me + r) % members, me).start())
        back_qk(h).wait()
        dm = dmqk[h]
        dm1 = jnp.where(off_far >= 1, dm, 0.0)
        dm2 = jnp.where(off_far >= 2, dm, 0.0)
        back = (
            w_cols[0] * dm[:, 0:tokens]
            + w_cols[1] * pltpu.roll(dm1, far - 1, 1)[:, 0:tokens]
            + w_cols[2] * pltpu.roll(dm2, far - 2, 1)[:, 0:tokens]
        )
        for m in range(members):
            sqk[m, h] = back[:, m * rows : m * rows + rows]
        loop(1, members, lambda r: out_qk(h, (me + r) % members, me).start())
        lane = lax.broadcasted_iota(jnp.int32, (LANES, LANES), 1)
        square = jnp.zeros((LANES, LANES), F32)
        for j, (d, sig) in enumerate(zip((dm, dm1, dm2), qk_signal(h))):
            tap = jnp.sum(d[:, 0:tokens] * sig, axis=1, keepdims=True)
            tall = jnp.concatenate([tap, jnp.zeros((LANES - 32, 1), F32)], axis=0)
            square = jnp.where(lane == j, tall, square)
        wmsg[group, h, :, LANES:] = square.T[0:8]
        wmsg[group, h, :, 0:LANES] = jnp.concatenate(sums + [jnp.zeros((5, HEAD_DIM), F32)], axis=0)
        for c in own_copies(h):
            c.start()

    def stage(i):
        @pl.when(i < hpd)
        def _():
            arrive(i)
            forward(i)

        @pl.when(i > 0)
        def _():
            finish(i - 1)

        @pl.when(i < hpd)
        def _():
            normalise(i)
            backward(i)

    loop(0, hpd + 1, stage)

    def w_copy(slot, g):
        return remote(wmsg.at[slot], wmsg.at[slot], w_send.at[g], w_recv.at[slot], device(g, me))

    def t_copy(m, slot):
        return remote(wtot.at[slot], wtot.at[slot], wt_send.at[m], wt_recv.at[slot], device(group, m))

    loop(1, groups, lambda r: w_copy(group, (group + r) % groups).start())
    loop(1, groups, lambda r: w_copy((group + groups - r) % groups, (group + groups - r) % groups).wait_recv())
    wtot[me] = lax.fori_loop(0, groups, lambda g, acc: acc + wmsg[g], jnp.zeros(wmsg.shape[1:], F32))
    loop(1, members, lambda r: t_copy((me + r) % members, me).start())

    def take(h):
        def one(r):
            m = (me + members - r) % members
            out_v(h, m, m).wait_recv()
            out_qk(h, m, m).wait_recv()

        loop(1, members, one)
        for c in own_copies(h):
            c.wait()

    loop(0, hpd, take)

    def take_taps(r):
        m = (me + members - r) % members
        t_copy(m, m).wait_recv()

    loop(1, members, take_taps)
    wt_ref[...] = wtot[...]

    def drain_members(r):
        m = (me + r) % members

        def one(h):
            o_copy(h, m, me).wait_send()
            out_v(h, m, me).wait_send()
            out_qk(h, m, me).wait_send()

        loop(0, hpd, one)
        t_copy(m, me).wait_send()

    loop(1, members, drain_members)
    loop(1, groups, lambda r: w_copy(group, (group + r) % groups).wait_send())

    def drain_states(h):
        for kind, refs in enumerate((keys, grads)):
            for part in range(2):
                each_state(kind, True, lambda r: state_copy(refs, kind, part, h, r).wait_send())

    loop(0, hpd, drain_states)


def unpack(hpd, v_any, qk_any, taps_ref, gp_any, gw_ref, v_ref, qk_ref, gp_ref, v_sem, qk_sem, out_sem):
    rows = gp_ref.shape[0]
    pairs = v_ref.shape[0] // 2
    wide = 2 * hpd * WIDTH

    def loads(i):
        at = pl.ds(2 * i, 2)
        return (
            pltpu.make_async_copy(v_any.at[at], v_ref.at[at], v_sem.at[i]),
            pltpu.make_async_copy(qk_any.at[at], qk_ref.at[at], qk_sem.at[i]),
        )

    def store(i):
        at = pl.ds(i * wide, wide)
        return pltpu.make_async_copy(gp_ref.at[:, at], gp_any.at[:, at], out_sem.at[i])

    for i in range(pairs):
        for c in loads(i):
            c.start()
    for n in range(HEADS):
        d, h = n // hpd, n % hpd
        first = WIDTH * n
        gw_ref[:, first : first + 32] = taps_ref[d, h, 0:3, LANES : LANES + 32]
        gw_ref[:, first + 32 : first + WIDTH] = taps_ref[d, h, 0:3, 0:LANES]
    for i in range(pairs):
        for c in loads(i):
            c.wait()
        for n in range(2 * hpd * i, 2 * hpd * (i + 1)):
            d, h = n // hpd, n % hpd
            first = WIDTH * n
            tall = jnp.concatenate([qk_ref[d, h], jnp.zeros((LANES - 32, rows), F32)], axis=0)
            gp_ref[:, first : first + 32] = tall.T[:, 0:32]
            gp_ref[:, first + 32 : first + WIDTH] = v_ref[d, h]
        store(i).start()
    for i in range(pairs):
        store(i).wait()


def on_device(sub, side, groups, projected, out_grads, conv_weight, doc_lengths):
    members = sub * side
    hpd = HEADS // members
    rows = projected.shape[0]
    tokens = rows * members
    reach = max(1, groups // 2)
    vmem = pltpu.VMEM
    dma = pltpu.SemaphoreType.DMA
    scratch = [
        vmem((members, hpd, rows, HEAD_DIM), F32),
        vmem((members, hpd, 32, rows), F32),
        vmem((hpd, tokens + 8, HEAD_DIM), F32),
        vmem((members + 1, hpd, 32, rows), F32),
        vmem((hpd, tokens, HEAD_DIM), F32),
        vmem((members, hpd, 8, HEAD_DIM), F32),
        vmem((members, hpd, 32, LANES), F32),
        vmem((tokens, LANES), jnp.int32),
        vmem((8, tokens), jnp.int32),
        vmem((hpd, tokens, HEAD_DIM), F32),
        vmem((hpd, 32, tokens), F32),
        vmem((hpd, tokens, 64), BF16),
        vmem((hpd, 64, tokens), BF16),
        vmem((hpd, 2, FEATS, tokens), BF16),
        vmem((hpd, 2, FEATS, tokens), BF16),
        vmem((hpd, tokens, LANES), F32),
        vmem((hpd, tokens, LANES), F32),
        vmem((hpd, tokens, LANES), F32),
        vmem((hpd, tokens, LANES), F32),
        vmem((reach + 1, hpd, FEATS, HEAD_DIM), F32),
        vmem((reach + 1, hpd, 8, 256), F32),
        vmem((reach + 1, hpd, FEATS, HEAD_DIM), F32),
        vmem((reach + 1, hpd, 8, 256), F32),
        vmem((hpd, 8, 256), F32),
        vmem((hpd, FEATS, HEAD_DIM), F32),
        vmem((hpd, tokens, tokens), F32),
        vmem((hpd, 2, tokens, tokens), BF16),
        vmem((hpd, tokens + 8, HEAD_DIM), F32),
        vmem((hpd, 32, tokens + LANES), F32),
        vmem((hpd, HEAD_DIM, tokens), F32),
        vmem((groups, hpd, 8, 2 * LANES), F32),
        vmem((members, hpd, 8, 2 * LANES), F32),
        dma((3, hpd, members)),
        dma((3, hpd, members)),
        dma((2, hpd, members)),
        dma((2, hpd)),
        dma((2, 2, hpd, reach + 1)),
        dma((2, 2, hpd, reach + 1)),
        dma((2, hpd)),
        dma((2, hpd)),
        dma((2, hpd, members)),
        dma((2, hpd, members)),
        dma((groups,)),
        dma((groups,)),
        dma((members,)),
        dma((members,)),
        dma((2, hpd)),
    ]
    spec = pl.BlockSpec(memory_space=pltpu.VMEM)
    returned = (members, hpd, rows, HEAD_DIM), (members, hpd, 32, rows), (members, hpd, 8, 2 * LANES)
    anywhere = pl.BlockSpec(memory_space=pl.ANY)
    values, columns, taps = pl.pallas_call(
        functools.partial(kernel, sub, side, groups, reach, "seq", "head"),
        out_shape=tuple(jax.ShapeDtypeStruct(shape, F32) for shape in returned),
        in_specs=[pl.BlockSpec(memory_space=pltpu.SMEM), spec, spec, spec],
        out_specs=(anywhere, anywhere, spec),
        scratch_shapes=scratch,
        compiler_params=pltpu.CompilerParams(
            collective_id=0, has_side_effects=True, vmem_limit_bytes=60 * 1024 * 1024
        ),
        name="layer_backward",
    )(doc_lengths, projected, out_grads, conv_weight)
    pairs = members // 2
    return pl.pallas_call(
        functools.partial(unpack, hpd),
        out_shape=(
            jax.ShapeDtypeStruct(projected.shape, F32),
            jax.ShapeDtypeStruct(conv_weight.shape, F32),
        ),
        in_specs=[anywhere, anywhere, spec],
        out_specs=(anywhere, spec),
        scratch_shapes=[
            vmem(returned[0], F32),
            vmem(returned[1], F32),
            vmem(projected.shape, F32),
            dma((pairs,)),
            dma((pairs,)),
            dma((pairs,)),
        ],
        compiler_params=pltpu.CompilerParams(vmem_limit_bytes=60 * 1024 * 1024),
        name="unpack_heads",
    )(values, columns, taps)


def solution(mesh):
    side = mesh.shape["head"]
    sub = max(1, MEMBERS // side)
    groups = mesh.shape["seq"] // sub
    return jax.shard_map(
        functools.partial(on_device, sub, side, groups),
        mesh=mesh,
        in_specs=(P(("seq", "head"), None), P(("seq", "head"), None), P(), P()),
        out_specs=(P(("seq", "head"), None), P()),
        check_vma=False,
    )
```

```python
import functools
import math

import jax
import jax.numpy as jnp
from jax import lax
from jax.experimental import pallas as pl
from jax.experimental.pallas import tpu as pltpu
from jax.sharding import PartitionSpec as P

KEY_DIM = 16
HEAD_DIM = 128
HEADS = 16
WIDTH = 2 * KEY_DIM + HEAD_DIM
MEMBERS = 8
FEATS = 160
BLOCK = 256
LANES = 128
MESH = pl.DeviceIdType.MESH
F32 = jnp.float32
BF16 = jnp.bfloat16


def halves(x):
    high = x.astype(BF16)
    return high, (x - high.astype(F32)).astype(BF16)


def dot(a, b, ca=1, cb=0):
    return lax.dot_general(a, b, (((ca,), (cb,)), ((), ())), preferred_element_type=F32)


def dot_halves(a, b, ca=1, cb=0):
    return dot(a[0], b[0], ca, cb) + (dot(a[0], b[1], ca, cb) + dot(a[1], b[0], ca, cb))


def features(x):
    twice = jnp.concatenate([x, x], axis=0)
    parts = [x * x * (1.0 / math.sqrt(2.0))]
    for d in range(1, 8):
        parts.append(x * twice[d : d + 16])
    parts.append(x[0:8] * x[8:16])
    parts.append(x)
    row = lax.broadcasted_iota(jnp.int32, (8, x.shape[1]), 0)
    parts.append((row == 0).astype(F32))
    return jnp.concatenate(parts, axis=0)


def features_pull(x, grad):
    twice = jnp.concatenate([x, x], axis=0)
    total = math.sqrt(2.0) * x * grad[0:16] + grad[136:152]
    for d in range(1, 8):
        g = grad[16 * d : 16 * d + 16]
        back = g * x
        back = jnp.concatenate([back, back], axis=0)[16 - d : 32 - d]
        total = total + g * twice[d : d + 16] + back
    g = grad[128:136]
    return total + jnp.concatenate([g * x[8:16], g * x[0:8]], axis=0)


def kernel(
    sub, side, groups, reach, seq_name, head_name,
    docs_ref, p_ref, o_ref, w_ref,
    rv, rqk, wt_ref,
    sv, sqk, v_buf, qk_buf, o_buf, wv_all, wqk_all,
    bcol, brow, vm, qkm, qrow, kst, qf, kf,
    num, den, gn_buf, gd_buf, gd_row,
    s_buf, n_buf, g_buf, gd_state, n_row, s_sum,
    u_buf, sc_buf, dmv, dmqk, dvt, wmsg, wtot,
    in_send, in_recv, halo_send, halo_recv, state_send, state_recv,
    back_send, back_recv, out_send, out_recv, w_send, w_recv, wt_send, wt_recv, own_sem,
):
    members = sub * side
    hpd = HEADS // members
    rows = p_ref.shape[0]
    tokens = rows * members
    total_len = tokens * groups
    ndoc = docs_ref.shape[0]
    seq = lax.axis_index(seq_name)
    group = seq // sub
    me = (seq % sub) * side + lax.axis_index(head_name)
    base = group * tokens
    nxt, prv = (group + 1) % groups, (group + groups - 1) % groups
    is_last = me == members - 1

    def device(g, m):
        return (g * sub + m // side, m % side)

    def remote(src, dst, send, recv, target):
        return pltpu.make_async_remote_copy(
            src_ref=src, dst_ref=dst, send_sem=send, recv_sem=recv, device_id=target, device_id_type=MESH
        )

    def loop(low, high, body):
        def step(r, _):
            body(r)
            return 0

        lax.fori_loop(low, high, step, 0)

    barrier = pltpu.get_barrier_semaphore()

    def greet(target):
        pl.semaphore_signal(barrier, inc=1, device_id=target, device_id_type=MESH)

    loop(1, members, lambda r: greet(device(group, (me + r) % members)))
    loop(1, groups, lambda r: greet(device((group + r) % groups, me)))

    @pl.when(is_last)
    def _():
        loop(0, members - 1, lambda m: greet(device(nxt, m)))

    @pl.when(jnp.logical_not(is_last))
    def _():
        greet(device(prv, members - 1))

    def pack(h):
        for d in range(members):
            first = WIDTH * (d * hpd + h)
            sv[d, h] = p_ref[:, first + 32 : first + WIDTH]

    for n in range(0, HEADS, 4):
        four = [p_ref[:, WIDTH * k : WIDTH * k + 32] for k in range(n, n + 4)]
        turned = jnp.concatenate(four, axis=1).T
        for k in range(4):
            sqk[(n + k) // hpd, (n + k) % hpd] = turned[32 * k : 32 * k + 32, :]
    pack(0)
    pl.semaphore_wait(barrier, members - 1 + groups - 1 + jnp.where(is_last, members - 1, 1))

    def qk_copy(h, m, slot):
        return remote(
            sqk.at[m, h], qk_buf.at[slot + 1, h], in_send.at[0, h, m], in_recv.at[0, h, slot], device(group, m)
        )

    def v_copy(h, m, slot):
        at = pl.ds(pl.multiple_of(rows * slot + 8, 8), rows)
        return remote(
            sv.at[m, h], v_buf.at[h, at, :], in_send.at[1, h, m], in_recv.at[1, h, slot], device(group, m)
        )

    def o_lanes(h, m):
        return pl.ds(pl.multiple_of((m * hpd + h) * HEAD_DIM, LANES), HEAD_DIM)

    def o_copy(h, m, slot):
        at = pl.ds(pl.multiple_of(rows * slot, rows), rows)
        return remote(
            o_ref.at[:, o_lanes(h, m)], o_buf.at[h, at, :], in_send.at[2, h, m], in_recv.at[2, h, slot],
            device(group, m),
        )

    def halo_qk(h, m, to):
        return remote(sqk.at[m, h], qk_buf.at[0, h], halo_send.at[0, h, m], halo_recv.at[0, h], device(to, m))

    def halo_v(h, m, to):
        return remote(
            sv.at[m, h, pl.ds(rows - 8, 8), :], v_buf.at[h, pl.ds(0, 8), :],
            halo_send.at[1, h, m], halo_recv.at[1, h], device(to, m),
        )

    def send_in(h):
        @pl.when(is_last)
        def _():
            def one(m):
                halo_qk(h, m, nxt).start()
                halo_v(h, m, nxt).start()

            loop(0, members, one)

        def one(r):
            m = (me + r) % members
            qk_copy(h, m, me).start()
            v_copy(h, m, me).start()

        loop(1, members, one)
        loop(1, members, lambda r: o_copy(h, (me + r) % members, me).start())

    send_in(0)
    for h in range(1, hpd):
        pack(h)
        send_in(h)

    def keep_own(h):
        qk_buf[me + 1, h] = sqk[me, h]
        v_buf[h, pl.ds(pl.multiple_of(rows * me + 8, 8), rows), :] = sv[me, h]
        o_buf[h, pl.ds(pl.multiple_of(rows * me, rows), rows), :] = o_ref[:, o_lanes(h, me)]

    loop(0, hpd, keep_own)

    for n in range(HEADS):
        d, h = n // hpd, n % hpd
        first = WIDTH * n
        tile = (first // LANES) * LANES
        off = first - tile
        square = jnp.concatenate([w_ref[:, tile : tile + LANES], jnp.zeros((LANES - 3, LANES), F32)], axis=0)
        wqk_all[d, h] = square.T[off : off + 32, :]
        wv_all[d, h, 0:3, :] = w_ref[:, first + 32 : first + WIDTH]

    starts = []
    run = jnp.int32(0)
    for i in range(ndoc):
        starts.append(run)
        run = run + docs_ref[i]

    def begin_of(pos):
        out = jnp.zeros_like(pos)
        for s in starts:
            out = jnp.where(s <= pos, s, out)
        return out

    bcol[...] = begin_of(base + lax.broadcasted_iota(jnp.int32, (tokens, LANES), 0))
    pos_row = base + lax.broadcasted_iota(jnp.int32, (8, tokens), 1)
    brow[...] = begin_of(pos_row)
    my_first = begin_of(base)
    my_last = begin_of(base + tokens - 1)

    pos = pos_row[0:1]
    beg = brow[0:1, :]
    off_row = pos - beg
    m1_row = (off_row >= 1).astype(F32)
    m2_row = (off_row >= 2).astype(F32)
    lead_row = (beg < base).astype(F32)
    tail_row = (beg == my_last).astype(F32)

    def qk_signal(h):
        sig = jnp.concatenate([qk_buf[m, h] for m in range(members + 1)], axis=1)
        return sig[:, LANES:], pltpu.roll(sig, 1, 1)[:, LANES:], pltpu.roll(sig, 2, 1)[:, LANES:]

    def taps_of(h):
        return [wqk_all[me, h, :, j : j + 1] for j in range(3)], [wv_all[me, h, j : j + 1, :] for j in range(3)]

    def q_of(h):
        return qkm[h, 0:16, :]

    def k_of(h):
        return qkm[h, 16:32, :]

    def state_copy(refs, kind, part, h, r):
        g = group + r if kind == 0 else group - r
        ref = refs[part]
        return remote(
            ref.at[0, h], ref.at[r, h], state_send.at[kind, part, h, r], state_recv.at[kind, part, h, r], device(g, me)
        )

    def ahead(kind, r):
        return group + r < groups if kind == 0 else group >= r

    def each_state(kind, to, body):
        def one(r):
            @pl.when(ahead(kind, r) if to else ahead(1 - kind, r))
            def _():
                body(r)

        loop(1, reach + 1, one)

    keys = (s_buf, n_buf)
    grads = (g_buf, gd_state)

    def arrive(h):
        def one(r):
            m = (me + members - r) % members
            qk_copy(h, m, m).wait_recv()
            v_copy(h, m, m).wait_recv()

        loop(1, members, one)
        halo_qk(h, me, prv).wait_recv()
        halo_v(h, me, prv).wait_recv()
        w_cols, w_rows = taps_of(h)
        s0, s1, s2 = qk_signal(h)
        qkm[h] = (w_cols[0] * s0 + w_cols[1] * (s1 * m1_row) + w_cols[2] * (s2 * m2_row)) * (KEY_DIM ** (-0.25))
        for b in range(tokens // BLOCK):
            t0 = b * BLOCK
            off = base + t0 + lax.broadcasted_iota(jnp.int32, (BLOCK, LANES), 0) - bcol[t0 : t0 + BLOCK, :]
            a0 = v_buf[h, t0 + 8 : t0 + 8 + BLOCK, :]
            a1 = jnp.where(off >= 1, v_buf[h, t0 + 7 : t0 + 7 + BLOCK, :], 0.0)
            a2 = jnp.where(off >= 2, v_buf[h, t0 + 6 : t0 + 6 + BLOCK, :], 0.0)
            vm[h, t0 : t0 + BLOCK, :] = w_rows[0] * a0 + w_rows[1] * a1 + w_rows[2] * a2
        k = k_of(h)
        kh, kl = halves(k)
        kst[h] = jnp.concatenate([kh, kl, kh, kl], axis=0)
        feat = halves(features(k) * tail_row)
        kf[h, 0], kf[h, 1] = feat
        ones = jnp.ones((8, tokens), BF16)
        norm = dot(ones, feat[0], 1, 1) + dot(ones, feat[1], 1, 1)
        n_buf[0, h] = jnp.concatenate([norm, jnp.zeros((8, 256 - FEATS), F32)], axis=1)
        each_state(0, True, lambda r: state_copy(keys, 0, 1, h, r).start())
        s_buf[0, h] = dot_halves(feat, halves(vm[h]))
        each_state(0, True, lambda r: state_copy(keys, 0, 0, h, r).start())

    def scores(h, i):
        wide = (i + 1) * BLOCK
        t0 = i * BLOCK
        u = 1.0 + dot(qrow[h, t0 : t0 + BLOCK, :], kst[h, :, 0:wide])
        s_pos = lax.broadcasted_iota(jnp.int32, (BLOCK, wide), 1)
        t_pos = t0 + lax.broadcasted_iota(jnp.int32, (BLOCK, wide), 0)
        begin = bcol[t0 : t0 + BLOCK, 0:1] - base
        allowed = (s_pos >= begin) & (s_pos <= t_pos)
        return jnp.where(allowed, u, 0.0), jnp.where(allowed, 0.5 + 0.5 * (u * u), 0.0)

    def forward(h):
        q = q_of(h)
        qh, ql = halves(q)
        qh, ql = qh.astype(F32), ql.astype(F32)
        qrow[h] = jnp.concatenate([qh, qh, ql, ql], axis=0).T.astype(BF16)
        qf[h, 0], qf[h, 1] = halves(features(q) * lead_row)
        vh, vl = halves(vm[h])
        both = jnp.concatenate([vh, vl], axis=1)
        for i in range(tokens // BLOCK):
            t0, wide = i * BLOCK, (i + 1) * BLOCK
            u, sc = scores(h, i)
            sh, sl = halves(sc)
            u_buf[h, t0 : t0 + BLOCK, 0:wide] = u
            sc_buf[h, 0, t0 : t0 + BLOCK, 0:wide] = sh
            sc_buf[h, 1, t0 : t0 + BLOCK, 0:wide] = sl
            wide_num = dot(sh, both[0:wide])
            num[h, t0 : t0 + BLOCK, :] = wide_num[:, 0:128] + (wide_num[:, 128:256] + dot(sl, vh[0:wide]))
            den[h, t0 : t0 + BLOCK, :] = jnp.broadcast_to(jnp.sum(sc, axis=1, keepdims=True), (BLOCK, LANES))

    def gather(kind, part, refs, total, h):
        total[h] = jnp.zeros(total.shape[1:], F32)

        def add(r):
            if kind == 0:
                weight = begin_of((group - r) * tokens + tokens - 1) == my_first
            else:
                weight = begin_of((group + r) * tokens) == my_last
            state_copy(refs, kind, part, h, r).wait_recv()
            total[h] = total[h] + weight.astype(F32) * refs[part][r, h]

        each_state(kind, False, add)

    def normalise(h):
        loop(1, members, lambda r: o_copy(h, (me + members - r) % members, (me + members - r) % members).wait_recv())
        gather(0, 1, keys, n_row, h)
        feat = (qf[h, 0], qf[h, 1])
        norm = halves(n_row[h, :, 0:FEATS])
        for i in range(tokens // BLOCK):
            t0 = i * BLOCK
            carried = dot_halves(norm, (feat[0][:, t0 : t0 + BLOCK], feat[1][:, t0 : t0 + BLOCK])).T[:, 0:1]
            inv = 1.0 / (den[h, t0 : t0 + BLOCK, :] + carried)
            den[h, t0 : t0 + BLOCK, :] = inv
            gn_buf[h, t0 : t0 + BLOCK, :] = o_buf[h, t0 : t0 + BLOCK, :] * inv
        g_buf[0, h] = dot_halves(feat, halves(gn_buf[h]))
        each_state(1, True, lambda r: state_copy(grads, 1, 0, h, r).start())
        gather(0, 0, keys, s_sum, h)
        left = halves(s_sum[h].T)
        for i in range(tokens // BLOCK):
            t0 = i * BLOCK
            carried = dot_halves(left, (feat[0][:, t0 : t0 + BLOCK], feat[1][:, t0 : t0 + BLOCK])).T
            attended = (num[h, t0 : t0 + BLOCK, :] + carried) * den[h, t0 : t0 + BLOCK, :]
            product = gn_buf[h, t0 : t0 + BLOCK, :] * attended
            gd = -jnp.sum(product, axis=1, keepdims=True)
            gd_buf[h, t0 : t0 + BLOCK, :] = jnp.broadcast_to(gd, (BLOCK, LANES))
            ones = jnp.ones((8, HEAD_DIM), BF16)
            high, low = halves(product)
            gd_row[h, :, t0 : t0 + BLOCK] = -(dot(ones, high, 1, 1) + dot(ones, low, 1, 1))
        norm = dot_halves(halves(gd_row[h]), feat, 1, 1)
        gd_state[0, h] = jnp.concatenate([norm, jnp.zeros((8, 256 - FEATS), F32)], axis=1)
        each_state(1, True, lambda r: state_copy(grads, 1, 1, h, r).start())

    def column(row):
        return row.T[0:FEATS, 0:1]

    far = tokens + LANES
    pos_far = base + lax.broadcasted_iota(jnp.int32, (1, far), 1)
    off_far = jnp.where(pos_far < total_len, pos_far - begin_of(pos_far), 0)

    def back_qk(h):
        return remote(
            dmqk.at[h, :, pl.ds(0, LANES)], dmqk.at[h, :, pl.ds(tokens, LANES)],
            back_send.at[0, h], back_recv.at[0, h], device(prv, me),
        )

    def back_v(h):
        return remote(
            dmv.at[h, pl.ds(0, 8), :], dmv.at[h, pl.ds(tokens, 8), :],
            back_send.at[1, h], back_recv.at[1, h], device(prv, me),
        )

    def out_qk(h, m, slot):
        return remote(sqk.at[m, h], rqk.at[slot, h], out_send.at[0, h, m], out_recv.at[0, h, slot], device(group, m))

    def out_v(h, m, slot):
        return remote(sv.at[m, h], rv.at[slot, h], out_send.at[1, h, m], out_recv.at[1, h, slot], device(group, m))

    def own_copies(h):
        return (
            pltpu.make_async_copy(sv.at[me, h], rv.at[me, h], own_sem.at[0, h]),
            pltpu.make_async_copy(sqk.at[me, h], rqk.at[me, h], own_sem.at[1, h]),
        )

    def backward(h):
        vh, vl = halves(vm[h])
        v_twice = jnp.concatenate([vh, vh], axis=1)
        qh, ql = halves(q_of(h))
        kh, kl = halves(k_of(h))
        q_both = jnp.concatenate([qh, ql], axis=0)
        k_both = jnp.concatenate([kh, kl], axis=0)
        dvt[h] = jnp.zeros((HEAD_DIM, tokens), F32)
        dmqk[h, 16:32, 0:tokens] = jnp.zeros((16, tokens), F32)
        for i in range(tokens // BLOCK):
            t0, wide = i * BLOCK, (i + 1) * BLOCK
            gn = gn_buf[h, t0 : t0 + BLOCK, :]
            gh, gl = halves(gn)
            ds = dot(jnp.concatenate([gh, gl], axis=1), v_twice[0:wide], 1, 1) + dot(gh, vl[0:wide], 1, 1)
            dh, dl = halves((ds + gd_buf[h, t0 : t0 + BLOCK, 0:1]) * u_buf[h, t0 : t0 + BLOCK, 0:wide])
            sh, sl = sc_buf[h, 0, t0 : t0 + BLOCK, 0:wide], sc_buf[h, 1, t0 : t0 + BLOCK, 0:wide]
            gth, gtl = halves(gn.T)
            dv = dot(jnp.concatenate([gth, gtl], axis=0), sh)
            dvt[h, :, 0:wide] += dv[0:128] + (dv[128:256] + dot(gth, sl))
            dk = dot(q_both[:, t0 : t0 + BLOCK], dh)
            dmqk[h, 16:32, 0:wide] += dk[0:16] + (dk[16:32] + dot(qh[:, t0 : t0 + BLOCK], dl))
            dq = dot(k_both[:, 0:wide], dh, 1, 1)
            dmqk[h, 0:16, t0 : t0 + BLOCK] = dq[0:16] + (dq[16:32] + dot(kh[:, 0:wide], dl, 1, 1))
        dqf = dot_halves(halves(s_sum[h]), halves(gn_buf[h]), 1, 1) + column(n_row[h]) * gd_row[h, 0:1, :]
        dmqk[h, 0:16, 0:tokens] += features_pull(q_of(h), dqf * lead_row)

    def finish(h):
        gather(1, 0, grads, s_sum, h)
        dv = dvt[h] + dot_halves(halves(s_sum[h].T), (kf[h, 0], kf[h, 1]))
        dmv[h, 0:tokens, :] = dv.T
        back_v(h).start()
        gather(1, 1, grads, n_row, h)
        dkf = dot_halves(halves(s_sum[h]), halves(vm[h]), 1, 1) + column(n_row[h])
        dmqk[h, 16:32, 0:tokens] += features_pull(k_of(h), dkf * tail_row)
        dmqk[h, :, 0:tokens] = dmqk[h, :, 0:tokens] * (KEY_DIM ** (-0.25))
        back_qk(h).start()

        def drain(r):
            m = (me + r) % members
            qk_copy(h, m, me).wait_send()
            v_copy(h, m, me).wait_send()

        loop(1, members, drain)

        @pl.when(is_last)
        def _():
            def one(m):
                halo_qk(h, m, nxt).wait_send()
                halo_v(h, m, nxt).wait_send()

            loop(0, members, one)

        w_cols, w_rows = taps_of(h)
        sums = [jnp.zeros((1, HEAD_DIM), F32) for _ in range(3)]
        for m in range(members):
            t0 = m * rows
            count = rows + 8
            if m == members - 1:
                back_v(h).wait()
            pcol = base + t0 + lax.broadcasted_iota(jnp.int32, (count, LANES), 0)
            off = jnp.where(pcol < total_len, pcol - begin_of(pcol), 0)
            d0 = dmv[h, t0 : t0 + count, :]
            d1 = jnp.where(off >= 1, d0, 0.0)
            d2 = jnp.where(off >= 2, d0, 0.0)
            sv[m, h] = w_rows[0] * d0[0:rows] + w_rows[1] * d1[1 : rows + 1] + w_rows[2] * d2[2 : rows + 2]
            for j, d in enumerate((d0, d1, d2)):
                past = v_buf[h, t0 + 8 - j : t0 + 8 - j + rows, :]
                sums[j] = sums[j] + jnp.sum(d[0:rows] * past, axis=0, keepdims=True)
        loop(1, members, lambda r: out_v(h, (me + r) % members, me).start())
        back_qk(h).wait()
        dm = dmqk[h]
        dm1 = jnp.where(off_far >= 1, dm, 0.0)
        dm2 = jnp.where(off_far >= 2, dm, 0.0)
        back = (
            w_cols[0] * dm[:, 0:tokens]
            + w_cols[1] * pltpu.roll(dm1, far - 1, 1)[:, 0:tokens]
            + w_cols[2] * pltpu.roll(dm2, far - 2, 1)[:, 0:tokens]
        )
        for m in range(members):
            sqk[m, h] = back[:, m * rows : m * rows + rows]
        loop(1, members, lambda r: out_qk(h, (me + r) % members, me).start())
        lane = lax.broadcasted_iota(jnp.int32, (LANES, LANES), 1)
        square = jnp.zeros((LANES, LANES), F32)
        for j, (d, sig) in enumerate(zip((dm, dm1, dm2), qk_signal(h))):
            tap = jnp.sum(d[:, 0:tokens] * sig, axis=1, keepdims=True)
            tall = jnp.concatenate([tap, jnp.zeros((LANES - 32, 1), F32)], axis=0)
            square = jnp.where(lane == j, tall, square)
        wmsg[group, h, :, LANES:] = square.T[0:8]
        wmsg[group, h, :, 0:LANES] = jnp.concatenate(sums + [jnp.zeros((5, HEAD_DIM), F32)], axis=0)
        for c in own_copies(h):
            c.start()

    def stage(i):
        @pl.when(i < hpd)
        def _():
            arrive(i)
            forward(i)

        @pl.when(i > 0)
        def _():
            finish(i - 1)

        @pl.when(i < hpd)
        def _():
            normalise(i)
            backward(i)

    loop(0, hpd + 1, stage)

    def w_copy(slot, g):
        return remote(wmsg.at[slot], wmsg.at[slot], w_send.at[g], w_recv.at[slot], device(g, me))

    def t_copy(m, slot):
        return remote(wtot.at[slot], wtot.at[slot], wt_send.at[m], wt_recv.at[slot], device(group, m))

    loop(1, groups, lambda r: w_copy(group, (group + r) % groups).start())
    loop(1, groups, lambda r: w_copy((group + groups - r) % groups, (group + groups - r) % groups).wait_recv())
    wtot[me] = lax.fori_loop(0, groups, lambda g, acc: acc + wmsg[g], jnp.zeros(wmsg.shape[1:], F32))
    loop(1, members, lambda r: t_copy((me + r) % members, me).start())

    def take(h):
        def one(r):
            m = (me + members - r) % members
            out_v(h, m, m).wait_recv()
            out_qk(h, m, m).wait_recv()

        loop(1, members, one)
        for c in own_copies(h):
            c.wait()

    loop(0, hpd, take)

    def take_taps(r):
        m = (me + members - r) % members
        t_copy(m, m).wait_recv()

    loop(1, members, take_taps)
    wt_ref[...] = wtot[...]

    def drain_members(r):
        m = (me + r) % members

        def one(h):
            o_copy(h, m, me).wait_send()
            out_v(h, m, me).wait_send()
            out_qk(h, m, me).wait_send()

        loop(0, hpd, one)
        t_copy(m, me).wait_send()

    loop(1, members, drain_members)
    loop(1, groups, lambda r: w_copy(group, (group + r) % groups).wait_send())

    def drain_states(h):
        for kind, refs in enumerate((keys, grads)):
            for part in range(2):
                each_state(kind, True, lambda r: state_copy(refs, kind, part, h, r).wait_send())

    loop(0, hpd, drain_states)


def unpack(hpd, v_any, qk_any, taps_ref, gp_any, gw_ref, v_ref, qk_ref, gp_ref, v_sem, qk_sem, out_sem):
    pairs = v_ref.shape[0] // 2
    wide = 2 * hpd * WIDTH

    def loads(i):
        at = pl.ds(2 * i, 2)
        return (
            pltpu.make_async_copy(v_any.at[at], v_ref.at[at], v_sem.at[i]),
            pltpu.make_async_copy(qk_any.at[at], qk_ref.at[at], qk_sem.at[i]),
        )

    def store(i):
        at = pl.ds(i * wide, wide)
        return pltpu.make_async_copy(gp_ref.at[:, at], gp_any.at[:, at], out_sem.at[i])

    for i in range(pairs):
        for c in loads(i):
            c.start()
    for n in range(HEADS):
        d, h = n // hpd, n % hpd
        first = WIDTH * n
        gw_ref[:, first : first + 32] = taps_ref[d, h, 0:3, LANES : LANES + 32]
        gw_ref[:, first + 32 : first + WIDTH] = taps_ref[d, h, 0:3, 0:LANES]
    for i in range(pairs):
        for c in loads(i):
            c.wait()
        for n in range(2 * hpd * i, 2 * hpd * (i + 1), 4):
            heads = [((n + k) // hpd, (n + k) % hpd) for k in range(4)]
            turned = jnp.concatenate([qk_ref[d, h] for d, h in heads], axis=0).T
            pieces = []
            for k, (d, h) in enumerate(heads):
                pieces += [turned[:, 32 * k : 32 * k + 32], v_ref[d, h]]
            gp_ref[:, WIDTH * n : WIDTH * (n + 4)] = jnp.concatenate(pieces, axis=1)
        store(i).start()
    for i in range(pairs):
        store(i).wait()


def on_device(sub, side, groups, projected, out_grads, conv_weight, doc_lengths):
    members = sub * side
    hpd = HEADS // members
    rows = projected.shape[0]
    tokens = rows * members
    reach = max(1, groups // 2)
    vmem = pltpu.VMEM
    dma = pltpu.SemaphoreType.DMA
    scratch = [
        vmem((members, hpd, rows, HEAD_DIM), F32),
        vmem((members, hpd, 32, rows), F32),
        vmem((hpd, tokens + 8, HEAD_DIM), F32),
        vmem((members + 1, hpd, 32, rows), F32),
        vmem((hpd, tokens, HEAD_DIM), F32),
        vmem((members, hpd, 8, HEAD_DIM), F32),
        vmem((members, hpd, 32, LANES), F32),
        vmem((tokens, LANES), jnp.int32),
        vmem((8, tokens), jnp.int32),
        vmem((hpd, tokens, HEAD_DIM), F32),
        vmem((hpd, 32, tokens), F32),
        vmem((hpd, tokens, 64), BF16),
        vmem((hpd, 64, tokens), BF16),
        vmem((hpd, 2, FEATS, tokens), BF16),
        vmem((hpd, 2, FEATS, tokens), BF16),
        vmem((hpd, tokens, LANES), F32),
        vmem((hpd, tokens, LANES), F32),
        vmem((hpd, tokens, LANES), F32),
        vmem((hpd, tokens, LANES), F32),
        vmem((hpd, 8, tokens), F32),
        vmem((reach + 1, hpd, FEATS, HEAD_DIM), F32),
        vmem((reach + 1, hpd, 8, 256), F32),
        vmem((reach + 1, hpd, FEATS, HEAD_DIM), F32),
        vmem((reach + 1, hpd, 8, 256), F32),
        vmem((hpd, 8, 256), F32),
        vmem((hpd, FEATS, HEAD_DIM), F32),
        vmem((hpd, tokens, tokens), F32),
        vmem((hpd, 2, tokens, tokens), BF16),
        vmem((hpd, tokens + 8, HEAD_DIM), F32),
        vmem((hpd, 32, tokens + LANES), F32),
        vmem((hpd, HEAD_DIM, tokens), F32),
        vmem((groups, hpd, 8, 2 * LANES), F32),
        vmem((members, hpd, 8, 2 * LANES), F32),
        dma((3, hpd, members)),
        dma((3, hpd, members)),
        dma((2, hpd, members)),
        dma((2, hpd)),
        dma((2, 2, hpd, reach + 1)),
        dma((2, 2, hpd, reach + 1)),
        dma((2, hpd)),
        dma((2, hpd)),
        dma((2, hpd, members)),
        dma((2, hpd, members)),
        dma((groups,)),
        dma((groups,)),
        dma((members,)),
        dma((members,)),
        dma((2, hpd)),
    ]
    spec = pl.BlockSpec(memory_space=pltpu.VMEM)
    returned = (members, hpd, rows, HEAD_DIM), (members, hpd, 32, rows), (members, hpd, 8, 2 * LANES)
    anywhere = pl.BlockSpec(memory_space=pl.ANY)
    values, columns, taps = pl.pallas_call(
        functools.partial(kernel, sub, side, groups, reach, "seq", "head"),
        out_shape=tuple(jax.ShapeDtypeStruct(shape, F32) for shape in returned),
        in_specs=[pl.BlockSpec(memory_space=pltpu.SMEM), spec, spec, spec],
        out_specs=(anywhere, anywhere, spec),
        scratch_shapes=scratch,
        compiler_params=pltpu.CompilerParams(
            collective_id=0, has_side_effects=True, vmem_limit_bytes=60 * 1024 * 1024
        ),
        name="layer_backward",
    )(doc_lengths, projected, out_grads, conv_weight)
    pairs = members // 2
    return pl.pallas_call(
        functools.partial(unpack, hpd),
        out_shape=(
            jax.ShapeDtypeStruct(projected.shape, F32),
            jax.ShapeDtypeStruct(conv_weight.shape, F32),
        ),
        in_specs=[anywhere, anywhere, spec],
        out_specs=(anywhere, spec),
        scratch_shapes=[
            vmem(returned[0], F32),
            vmem(returned[1], F32),
            vmem(projected.shape, F32),
            dma((pairs,)),
            dma((pairs,)),
            dma((pairs,)),
        ],
        compiler_params=pltpu.CompilerParams(vmem_limit_bytes=60 * 1024 * 1024),
        name="unpack_heads",
    )(values, columns, taps)


def solution(mesh):
    side = mesh.shape["head"]
    sub = max(1, MEMBERS // side)
    groups = mesh.shape["seq"] // sub
    return jax.shard_map(
        functools.partial(on_device, sub, side, groups),
        mesh=mesh,
        in_specs=(P(("seq", "head"), None), P(("seq", "head"), None), P(), P()),
        out_specs=(P(("seq", "head"), None), P()),
        check_vma=False,
    )
```

```python
import functools
import math

import jax
import jax.numpy as jnp
from jax import lax
from jax.experimental import pallas as pl
from jax.experimental.pallas import tpu as pltpu
from jax.sharding import PartitionSpec as P

KEY_DIM = 16
HEAD_DIM = 128
HEADS = 16
WIDTH = 2 * KEY_DIM + HEAD_DIM
MEMBERS = 8
FEATS = 160
BLOCK = 256
LANES = 128
MESH = pl.DeviceIdType.MESH
F32 = jnp.float32
BF16 = jnp.bfloat16


def halves(x):
    high = x.astype(BF16)
    return high, (x - high.astype(F32)).astype(BF16)


def dot(a, b, ca=1, cb=0):
    return lax.dot_general(a, b, (((ca,), (cb,)), ((), ())), preferred_element_type=F32)


def dot_halves(a, b, ca=1, cb=0):
    return dot(a[0], b[0], ca, cb) + (dot(a[0], b[1], ca, cb) + dot(a[1], b[0], ca, cb))


def features(x):
    twice = jnp.concatenate([x, x], axis=0)
    parts = [x * x * (1.0 / math.sqrt(2.0))]
    for d in range(1, 8):
        parts.append(x * twice[d : d + 16])
    parts.append(x[0:8] * x[8:16])
    parts.append(x)
    row = lax.broadcasted_iota(jnp.int32, (8, x.shape[1]), 0)
    parts.append((row == 0).astype(F32))
    return jnp.concatenate(parts, axis=0)


def features_pull(x, grad):
    twice = jnp.concatenate([x, x], axis=0)
    total = math.sqrt(2.0) * x * grad[0:16] + grad[136:152]
    for d in range(1, 8):
        g = grad[16 * d : 16 * d + 16]
        back = g * x
        back = jnp.concatenate([back, back], axis=0)[16 - d : 32 - d]
        total = total + g * twice[d : d + 16] + back
    g = grad[128:136]
    return total + jnp.concatenate([g * x[8:16], g * x[0:8]], axis=0)


def kernel(
    sub, side, groups, reach, seq_name, head_name,
    docs_ref, p_ref, o_ref, w_ref,
    rv, rqk, wt_ref,
    sv, sqk, v_buf, qk_buf, o_buf, wv_all, wqk_all,
    bcol, brow, vm, qkm, qrow, kst, qf, kf,
    num, den, gn_buf, gd_buf, gd_row,
    s_buf, n_buf, g_buf, gd_state, n_row, s_sum,
    u_buf, sc_buf, dmv, dmqk, dvt, wmsg, wtot,
    in_send, in_recv, halo_send, halo_recv, state_send, state_recv,
    back_send, back_recv, out_send, out_recv, w_send, w_recv, wt_send, wt_recv, own_sem,
):
    members = sub * side
    hpd = HEADS // members
    rows = p_ref.shape[0]
    tokens = rows * members
    total_len = tokens * groups
    ndoc = docs_ref.shape[0]
    seq = lax.axis_index(seq_name)
    group = seq // sub
    me = (seq % sub) * side + lax.axis_index(head_name)
    base = group * tokens
    nxt, prv = (group + 1) % groups, (group + groups - 1) % groups
    is_last = me == members - 1

    def device(g, m):
        return (g * sub + m // side, m % side)

    def remote(src, dst, send, recv, target):
        return pltpu.make_async_remote_copy(
            src_ref=src, dst_ref=dst, send_sem=send, recv_sem=recv, device_id=target, device_id_type=MESH
        )

    def loop(low, high, body):
        def step(r, _):
            body(r)
            return 0

        lax.fori_loop(low, high, step, 0)

    barrier = pltpu.get_barrier_semaphore()

    def greet(target):
        pl.semaphore_signal(barrier, inc=1, device_id=target, device_id_type=MESH)

    loop(1, members, lambda r: greet(device(group, (me + r) % members)))
    loop(1, groups, lambda r: greet(device((group + r) % groups, me)))

    @pl.when(is_last)
    def _():
        loop(0, members - 1, lambda m: greet(device(nxt, m)))

    @pl.when(jnp.logical_not(is_last))
    def _():
        greet(device(prv, members - 1))

    def pack(h):
        for d in range(members):
            first = WIDTH * (d * hpd + h)
            sv[d, h] = p_ref[:, first + 32 : first + WIDTH]
        for d in range(0, members, 4):
            firsts = [WIDTH * (k * hpd + h) for k in range(d, d + 4)]
            turned = jnp.concatenate([p_ref[:, a : a + 32] for a in firsts], axis=1).T
            for k in range(4):
                sqk[d + k, h] = turned[32 * k : 32 * k + 32, :]

    pack(0)
    pl.semaphore_wait(barrier, members - 1 + groups - 1 + jnp.where(is_last, members - 1, 1))

    def qk_copy(h, m, slot):
        return remote(
            sqk.at[m, h], qk_buf.at[slot + 1, h], in_send.at[0, h, m], in_recv.at[0, h, slot], device(group, m)
        )

    def v_copy(h, m, slot):
        at = pl.ds(pl.multiple_of(rows * slot + 8, 8), rows)
        return remote(
            sv.at[m, h], v_buf.at[h, at, :], in_send.at[1, h, m], in_recv.at[1, h, slot], device(group, m)
        )

    def o_lanes(h, m):
        return pl.ds(pl.multiple_of((m * hpd + h) * HEAD_DIM, LANES), HEAD_DIM)

    def o_copy(h, m, slot):
        at = pl.ds(pl.multiple_of(rows * slot, rows), rows)
        return remote(
            o_ref.at[:, o_lanes(h, m)], o_buf.at[h, at, :], in_send.at[2, h, m], in_recv.at[2, h, slot],
            device(group, m),
        )

    def halo_qk(h, m, to):
        return remote(sqk.at[m, h], qk_buf.at[0, h], halo_send.at[0, h, m], halo_recv.at[0, h], device(to, m))

    def halo_v(h, m, to):
        return remote(
            sv.at[m, h, pl.ds(rows - 8, 8), :], v_buf.at[h, pl.ds(0, 8), :],
            halo_send.at[1, h, m], halo_recv.at[1, h], device(to, m),
        )

    def send_in(h):
        @pl.when(is_last)
        def _():
            def one(m):
                halo_qk(h, m, nxt).start()
                halo_v(h, m, nxt).start()

            loop(0, members, one)

        def one(r):
            m = (me + r) % members
            qk_copy(h, m, me).start()
            v_copy(h, m, me).start()

        loop(1, members, one)
        loop(1, members, lambda r: o_copy(h, (me + r) % members, me).start())

    send_in(0)
    for h in range(1, hpd):
        pack(h)
        send_in(h)

    def keep_own(h):
        qk_buf[me + 1, h] = sqk[me, h]
        v_buf[h, pl.ds(pl.multiple_of(rows * me + 8, 8), rows), :] = sv[me, h]
        o_buf[h, pl.ds(pl.multiple_of(rows * me, rows), rows), :] = o_ref[:, o_lanes(h, me)]

    loop(0, hpd, keep_own)

    for n in range(HEADS):
        d, h = n // hpd, n % hpd
        first = WIDTH * n
        tile = (first // LANES) * LANES
        off = first - tile
        square = jnp.concatenate([w_ref[:, tile : tile + LANES], jnp.zeros((LANES - 3, LANES), F32)], axis=0)
        wqk_all[d, h] = square.T[off : off + 32, :]
        wv_all[d, h, 0:3, :] = w_ref[:, first + 32 : first + WIDTH]

    starts = []
    run = jnp.int32(0)
    for i in range(ndoc):
        starts.append(run)
        run = run + docs_ref[i]

    def begin_of(pos):
        out = jnp.zeros_like(pos)
        for s in starts:
            out = jnp.where(s <= pos, s, out)
        return out

    bcol[...] = begin_of(base + lax.broadcasted_iota(jnp.int32, (tokens, LANES), 0))
    pos_row = base + lax.broadcasted_iota(jnp.int32, (8, tokens), 1)
    brow[...] = begin_of(pos_row)
    my_first = begin_of(base)
    my_last = begin_of(base + tokens - 1)

    pos = pos_row[0:1]
    beg = brow[0:1, :]
    off_row = pos - beg
    m1_row = (off_row >= 1).astype(F32)
    m2_row = (off_row >= 2).astype(F32)
    lead_row = (beg < base).astype(F32)
    tail_row = (beg == my_last).astype(F32)

    def qk_signal(h):
        sig = jnp.concatenate([qk_buf[m, h] for m in range(members + 1)], axis=1)
        return sig[:, LANES:], pltpu.roll(sig, 1, 1)[:, LANES:], pltpu.roll(sig, 2, 1)[:, LANES:]

    def taps_of(h):
        return [wqk_all[me, h, :, j : j + 1] for j in range(3)], [wv_all[me, h, j : j + 1, :] for j in range(3)]

    def q_of(h):
        return qkm[h, 0:16, :]

    def k_of(h):
        return qkm[h, 16:32, :]

    def state_copy(refs, kind, part, h, r):
        g = group + r if kind == 0 else group - r
        ref = refs[part]
        return remote(
            ref.at[0, h], ref.at[r, h], state_send.at[kind, part, h, r], state_recv.at[kind, part, h, r], device(g, me)
        )

    def ahead(kind, r):
        return group + r < groups if kind == 0 else group >= r

    def each_state(kind, to, body):
        def one(r):
            @pl.when(ahead(kind, r) if to else ahead(1 - kind, r))
            def _():
                body(r)

        loop(1, reach + 1, one)

    keys = (s_buf, n_buf)
    grads = (g_buf, gd_state)

    def arrive(h):
        def one(r):
            m = (me + members - r) % members
            qk_copy(h, m, m).wait_recv()
            v_copy(h, m, m).wait_recv()

        loop(1, members, one)
        halo_qk(h, me, prv).wait_recv()
        halo_v(h, me, prv).wait_recv()
        w_cols, w_rows = taps_of(h)
        s0, s1, s2 = qk_signal(h)
        qkm[h] = (w_cols[0] * s0 + w_cols[1] * (s1 * m1_row) + w_cols[2] * (s2 * m2_row)) * (KEY_DIM ** (-0.25))
        for b in range(tokens // BLOCK):
            t0 = b * BLOCK
            off = base + t0 + lax.broadcasted_iota(jnp.int32, (BLOCK, LANES), 0) - bcol[t0 : t0 + BLOCK, :]
            a0 = v_buf[h, t0 + 8 : t0 + 8 + BLOCK, :]
            a1 = jnp.where(off >= 1, v_buf[h, t0 + 7 : t0 + 7 + BLOCK, :], 0.0)
            a2 = jnp.where(off >= 2, v_buf[h, t0 + 6 : t0 + 6 + BLOCK, :], 0.0)
            vm[h, t0 : t0 + BLOCK, :] = w_rows[0] * a0 + w_rows[1] * a1 + w_rows[2] * a2
        k = k_of(h)
        kh, kl = halves(k)
        kst[h] = jnp.concatenate([kh, kl, kh, kl], axis=0)
        feat = halves(features(k) * tail_row)
        kf[h, 0], kf[h, 1] = feat
        ones = jnp.ones((8, tokens), BF16)
        norm = dot(ones, feat[0], 1, 1) + dot(ones, feat[1], 1, 1)
        n_buf[0, h] = jnp.concatenate([norm, jnp.zeros((8, 256 - FEATS), F32)], axis=1)
        each_state(0, True, lambda r: state_copy(keys, 0, 1, h, r).start())
        s_buf[0, h] = dot_halves(feat, halves(vm[h]))
        each_state(0, True, lambda r: state_copy(keys, 0, 0, h, r).start())

    def scores(h, i):
        wide = (i + 1) * BLOCK
        t0 = i * BLOCK
        u = 1.0 + dot(qrow[h, t0 : t0 + BLOCK, :], kst[h, :, 0:wide])
        s_pos = lax.broadcasted_iota(jnp.int32, (BLOCK, wide), 1)
        t_pos = t0 + lax.broadcasted_iota(jnp.int32, (BLOCK, wide), 0)
        begin = bcol[t0 : t0 + BLOCK, 0:1] - base
        allowed = (s_pos >= begin) & (s_pos <= t_pos)
        return jnp.where(allowed, u, 0.0), jnp.where(allowed, 0.5 + 0.5 * (u * u), 0.0)

    def forward(h):
        q = q_of(h)
        qh, ql = halves(q)
        qh, ql = qh.astype(F32), ql.astype(F32)
        qrow[h] = jnp.concatenate([qh, qh, ql, ql], axis=0).T.astype(BF16)
        qf[h, 0], qf[h, 1] = halves(features(q) * lead_row)
        vh, vl = halves(vm[h])
        both = jnp.concatenate([vh, vl], axis=1)
        for i in range(tokens // BLOCK):
            t0, wide = i * BLOCK, (i + 1) * BLOCK
            u, sc = scores(h, i)
            sh, sl = halves(sc)
            u_buf[h, t0 : t0 + BLOCK, 0:wide] = u
            sc_buf[h, 0, t0 : t0 + BLOCK, 0:wide] = sh
            sc_buf[h, 1, t0 : t0 + BLOCK, 0:wide] = sl
            wide_num = dot(sh, both[0:wide])
            num[h, t0 : t0 + BLOCK, :] = wide_num[:, 0:128] + (wide_num[:, 128:256] + dot(sl, vh[0:wide]))
            den[h, t0 : t0 + BLOCK, :] = jnp.broadcast_to(jnp.sum(sc, axis=1, keepdims=True), (BLOCK, LANES))

    def gather(kind, part, refs, total, h):
        total[h] = jnp.zeros(total.shape[1:], F32)

        def add(r):
            if kind == 0:
                weight = begin_of((group - r) * tokens + tokens - 1) == my_first
            else:
                weight = begin_of((group + r) * tokens) == my_last
            state_copy(refs, kind, part, h, r).wait_recv()
            total[h] = total[h] + weight.astype(F32) * refs[part][r, h]

        each_state(kind, False, add)

    def normalise(h):
        loop(1, members, lambda r: o_copy(h, (me + members - r) % members, (me + members - r) % members).wait_recv())
        gather(0, 1, keys, n_row, h)
        feat = (qf[h, 0], qf[h, 1])
        norm = halves(n_row[h, :, 0:FEATS])
        for i in range(tokens // BLOCK):
            t0 = i * BLOCK
            carried = dot_halves(norm, (feat[0][:, t0 : t0 + BLOCK], feat[1][:, t0 : t0 + BLOCK])).T[:, 0:1]
            inv = 1.0 / (den[h, t0 : t0 + BLOCK, :] + carried)
            den[h, t0 : t0 + BLOCK, :] = inv
            gn_buf[h, t0 : t0 + BLOCK, :] = o_buf[h, t0 : t0 + BLOCK, :] * inv
        g_buf[0, h] = dot_halves(feat, halves(gn_buf[h]))
        each_state(1, True, lambda r: state_copy(grads, 1, 0, h, r).start())
        gather(0, 0, keys, s_sum, h)
        left = halves(s_sum[h].T)
        for i in range(tokens // BLOCK):
            t0 = i * BLOCK
            carried = dot_halves(left, (feat[0][:, t0 : t0 + BLOCK], feat[1][:, t0 : t0 + BLOCK])).T
            attended = (num[h, t0 : t0 + BLOCK, :] + carried) * den[h, t0 : t0 + BLOCK, :]
            product = gn_buf[h, t0 : t0 + BLOCK, :] * attended
            gd = -jnp.sum(product, axis=1, keepdims=True)
            gd_buf[h, t0 : t0 + BLOCK, :] = jnp.broadcast_to(gd, (BLOCK, LANES))
            ones = jnp.ones((8, HEAD_DIM), BF16)
            high, low = halves(product)
            gd_row[h, :, t0 : t0 + BLOCK] = -(dot(ones, high, 1, 1) + dot(ones, low, 1, 1))
        norm = dot_halves(halves(gd_row[h]), feat, 1, 1)
        gd_state[0, h] = jnp.concatenate([norm, jnp.zeros((8, 256 - FEATS), F32)], axis=1)
        each_state(1, True, lambda r: state_copy(grads, 1, 1, h, r).start())

    def column(row):
        return row.T[0:FEATS, 0:1]

    far = tokens + LANES
    pos_far = base + lax.broadcasted_iota(jnp.int32, (1, far), 1)
    off_far = jnp.where(pos_far < total_len, pos_far - begin_of(pos_far), 0)

    def back_qk(h):
        return remote(
            dmqk.at[h, :, pl.ds(0, LANES)], dmqk.at[h, :, pl.ds(tokens, LANES)],
            back_send.at[0, h], back_recv.at[0, h], device(prv, me),
        )

    def back_v(h):
        return remote(
            dmv.at[h, pl.ds(0, 8), :], dmv.at[h, pl.ds(tokens, 8), :],
            back_send.at[1, h], back_recv.at[1, h], device(prv, me),
        )

    def out_qk(h, m, slot):
        return remote(sqk.at[m, h], rqk.at[slot, h], out_send.at[0, h, m], out_recv.at[0, h, slot], device(group, m))

    def out_v(h, m, slot):
        return remote(sv.at[m, h], rv.at[slot, h], out_send.at[1, h, m], out_recv.at[1, h, slot], device(group, m))

    def own_copies(h):
        return (
            pltpu.make_async_copy(sv.at[me, h], rv.at[me, h], own_sem.at[0, h]),
            pltpu.make_async_copy(sqk.at[me, h], rqk.at[me, h], own_sem.at[1, h]),
        )

    def backward(h):
        vh, vl = halves(vm[h])
        v_twice = jnp.concatenate([vh, vh], axis=1)
        qh, ql = halves(q_of(h))
        kh, kl = halves(k_of(h))
        q_both = jnp.concatenate([qh, ql], axis=0)
        k_both = jnp.concatenate([kh, kl], axis=0)
        dvt[h] = jnp.zeros((HEAD_DIM, tokens), F32)
        dmqk[h, 16:32, 0:tokens] = jnp.zeros((16, tokens), F32)
        for i in range(tokens // BLOCK):
            t0, wide = i * BLOCK, (i + 1) * BLOCK
            gn = gn_buf[h, t0 : t0 + BLOCK, :]
            gh, gl = halves(gn)
            ds = dot(jnp.concatenate([gh, gl], axis=1), v_twice[0:wide], 1, 1) + dot(gh, vl[0:wide], 1, 1)
            dh, dl = halves((ds + gd_buf[h, t0 : t0 + BLOCK, 0:1]) * u_buf[h, t0 : t0 + BLOCK, 0:wide])
            sh, sl = sc_buf[h, 0, t0 : t0 + BLOCK, 0:wide], sc_buf[h, 1, t0 : t0 + BLOCK, 0:wide]
            gth, gtl = halves(gn.T)
            dv = dot(jnp.concatenate([gth, gtl], axis=0), sh)
            dvt[h, :, 0:wide] += dv[0:128] + (dv[128:256] + dot(gth, sl))
            dk = dot(q_both[:, t0 : t0 + BLOCK], dh)
            dmqk[h, 16:32, 0:wide] += dk[0:16] + (dk[16:32] + dot(qh[:, t0 : t0 + BLOCK], dl))
            dq = dot(k_both[:, 0:wide], dh, 1, 1)
            dmqk[h, 0:16, t0 : t0 + BLOCK] = dq[0:16] + (dq[16:32] + dot(kh[:, 0:wide], dl, 1, 1))
        dqf = dot_halves(halves(s_sum[h]), halves(gn_buf[h]), 1, 1) + column(n_row[h]) * gd_row[h, 0:1, :]
        dmqk[h, 0:16, 0:tokens] += features_pull(q_of(h), dqf * lead_row)

    def finish(h):
        gather(1, 0, grads, s_sum, h)
        dv = dvt[h] + dot_halves(halves(s_sum[h].T), (kf[h, 0], kf[h, 1]))
        dmv[h, 0:tokens, :] = dv.T
        back_v(h).start()
        gather(1, 1, grads, n_row, h)
        dkf = dot_halves(halves(s_sum[h]), halves(vm[h]), 1, 1) + column(n_row[h])
        dmqk[h, 16:32, 0:tokens] += features_pull(k_of(h), dkf * tail_row)
        dmqk[h, :, 0:tokens] = dmqk[h, :, 0:tokens] * (KEY_DIM ** (-0.25))
        back_qk(h).start()

        def drain(r):
            m = (me + r) % members
            qk_copy(h, m, me).wait_send()
            v_copy(h, m, me).wait_send()

        loop(1, members, drain)

        @pl.when(is_last)
        def _():
            def one(m):
                halo_qk(h, m, nxt).wait_send()
                halo_v(h, m, nxt).wait_send()

            loop(0, members, one)

        w_cols, w_rows = taps_of(h)
        sums = [jnp.zeros((1, HEAD_DIM), F32) for _ in range(3)]
        for m in range(members):
            t0 = m * rows
            count = rows + 8
            if m == members - 1:
                back_v(h).wait()
            pcol = base + t0 + lax.broadcasted_iota(jnp.int32, (count, LANES), 0)
            off = jnp.where(pcol < total_len, pcol - begin_of(pcol), 0)
            d0 = dmv[h, t0 : t0 + count, :]
            d1 = jnp.where(off >= 1, d0, 0.0)
            d2 = jnp.where(off >= 2, d0, 0.0)
            sv[m, h] = w_rows[0] * d0[0:rows] + w_rows[1] * d1[1 : rows + 1] + w_rows[2] * d2[2 : rows + 2]
            for j, d in enumerate((d0, d1, d2)):
                past = v_buf[h, t0 + 8 - j : t0 + 8 - j + rows, :]
                sums[j] = sums[j] + jnp.sum(d[0:rows] * past, axis=0, keepdims=True)
        loop(1, members, lambda r: out_v(h, (me + r) % members, me).start())
        back_qk(h).wait()
        dm = dmqk[h]
        dm1 = jnp.where(off_far >= 1, dm, 0.0)
        dm2 = jnp.where(off_far >= 2, dm, 0.0)
        back = (
            w_cols[0] * dm[:, 0:tokens]
            + w_cols[1] * pltpu.roll(dm1, far - 1, 1)[:, 0:tokens]
            + w_cols[2] * pltpu.roll(dm2, far - 2, 1)[:, 0:tokens]
        )
        for m in range(members):
            sqk[m, h] = back[:, m * rows : m * rows + rows]
        loop(1, members, lambda r: out_qk(h, (me + r) % members, me).start())
        lane = lax.broadcasted_iota(jnp.int32, (LANES, LANES), 1)
        square = jnp.zeros((LANES, LANES), F32)
        for j, (d, sig) in enumerate(zip((dm, dm1, dm2), qk_signal(h))):
            tap = jnp.sum(d[:, 0:tokens] * sig, axis=1, keepdims=True)
            tall = jnp.concatenate([tap, jnp.zeros((LANES - 32, 1), F32)], axis=0)
            square = jnp.where(lane == j, tall, square)
        wmsg[group, h, :, LANES:] = square.T[0:8]
        wmsg[group, h, :, 0:LANES] = jnp.concatenate(sums + [jnp.zeros((5, HEAD_DIM), F32)], axis=0)
        for c in own_copies(h):
            c.start()

    def stage(i):
        @pl.when(i < hpd)
        def _():
            arrive(i)
            forward(i)

        @pl.when(i > 0)
        def _():
            finish(i - 1)

        @pl.when(i < hpd)
        def _():
            normalise(i)
            backward(i)

    loop(0, hpd + 1, stage)

    def w_copy(slot, g):
        return remote(wmsg.at[slot], wmsg.at[slot], w_send.at[g], w_recv.at[slot], device(g, me))

    def t_copy(m, slot):
        return remote(wtot.at[slot], wtot.at[slot], wt_send.at[m], wt_recv.at[slot], device(group, m))

    loop(1, groups, lambda r: w_copy(group, (group + r) % groups).start())
    loop(1, groups, lambda r: w_copy((group + groups - r) % groups, (group + groups - r) % groups).wait_recv())
    wtot[me] = lax.fori_loop(0, groups, lambda g, acc: acc + wmsg[g], jnp.zeros(wmsg.shape[1:], F32))
    loop(1, members, lambda r: t_copy((me + r) % members, me).start())

    def take(h):
        def one(r):
            m = (me + members - r) % members
            out_v(h, m, m).wait_recv()
            out_qk(h, m, m).wait_recv()

        loop(1, members, one)
        for c in own_copies(h):
            c.wait()

    loop(0, hpd, take)

    def take_taps(r):
        m = (me + members - r) % members
        t_copy(m, m).wait_recv()

    loop(1, members, take_taps)
    wt_ref[...] = wtot[...]

    def drain_members(r):
        m = (me + r) % members

        def one(h):
            o_copy(h, m, me).wait_send()
            out_v(h, m, me).wait_send()
            out_qk(h, m, me).wait_send()

        loop(0, hpd, one)
        t_copy(m, me).wait_send()

    loop(1, members, drain_members)
    loop(1, groups, lambda r: w_copy(group, (group + r) % groups).wait_send())

    def drain_states(h):
        for kind, refs in enumerate((keys, grads)):
            for part in range(2):
                each_state(kind, True, lambda r: state_copy(refs, kind, part, h, r).wait_send())

    loop(0, hpd, drain_states)


def unpack(hpd, v_any, qk_any, taps_ref, gp_any, gw_ref, v_ref, qk_ref, gp_ref, v_sem, qk_sem, out_sem):
    pairs = v_ref.shape[0] // 2
    wide = 2 * hpd * WIDTH

    def loads(i):
        at = pl.ds(2 * i, 2)
        return (
            pltpu.make_async_copy(v_any.at[at], v_ref.at[at], v_sem.at[i]),
            pltpu.make_async_copy(qk_any.at[at], qk_ref.at[at], qk_sem.at[i]),
        )

    def store(i):
        at = pl.ds(i * wide, wide)
        return pltpu.make_async_copy(gp_ref.at[:, at], gp_any.at[:, at], out_sem.at[i])

    for i in range(pairs):
        for c in loads(i):
            c.start()
    for n in range(HEADS):
        d, h = n // hpd, n % hpd
        first = WIDTH * n
        gw_ref[:, first : first + 32] = taps_ref[d, h, 0:3, LANES : LANES + 32]
        gw_ref[:, first + 32 : first + WIDTH] = taps_ref[d, h, 0:3, 0:LANES]
    for i in range(pairs):
        for c in loads(i):
            c.wait()
        for n in range(2 * hpd * i, 2 * hpd * (i + 1), 4):
            heads = [((n + k) // hpd, (n + k) % hpd) for k in range(4)]
            turned = jnp.concatenate([qk_ref[d, h] for d, h in heads], axis=0).T
            pieces = []
            for k, (d, h) in enumerate(heads):
                pieces += [turned[:, 32 * k : 32 * k + 32], v_ref[d, h]]
            gp_ref[:, WIDTH * n : WIDTH * (n + 4)] = jnp.concatenate(pieces, axis=1)
        store(i).start()
    for i in range(pairs):
        store(i).wait()


def on_device(sub, side, groups, projected, out_grads, conv_weight, doc_lengths):
    members = sub * side
    hpd = HEADS // members
    rows = projected.shape[0]
    tokens = rows * members
    reach = max(1, groups // 2)
    vmem = pltpu.VMEM
    dma = pltpu.SemaphoreType.DMA
    scratch = [
        vmem((members, hpd, rows, HEAD_DIM), F32),
        vmem((members, hpd, 32, rows), F32),
        vmem((hpd, tokens + 8, HEAD_DIM), F32),
        vmem((members + 1, hpd, 32, rows), F32),
        vmem((hpd, tokens, HEAD_DIM), F32),
        vmem((members, hpd, 8, HEAD_DIM), F32),
        vmem((members, hpd, 32, LANES), F32),
        vmem((tokens, LANES), jnp.int32),
        vmem((8, tokens), jnp.int32),
        vmem((hpd, tokens, HEAD_DIM), F32),
        vmem((hpd, 32, tokens), F32),
        vmem((hpd, tokens, 64), BF16),
        vmem((hpd, 64, tokens), BF16),
        vmem((hpd, 2, FEATS, tokens), BF16),
        vmem((hpd, 2, FEATS, tokens), BF16),
        vmem((hpd, tokens, LANES), F32),
        vmem((hpd, tokens, LANES), F32),
        vmem((hpd, tokens, LANES), F32),
        vmem((hpd, tokens, LANES), F32),
        vmem((hpd, 8, tokens), F32),
        vmem((reach + 1, hpd, FEATS, HEAD_DIM), F32),
        vmem((reach + 1, hpd, 8, 256), F32),
        vmem((reach + 1, hpd, FEATS, HEAD_DIM), F32),
        vmem((reach + 1, hpd, 8, 256), F32),
        vmem((hpd, 8, 256), F32),
        vmem((hpd, FEATS, HEAD_DIM), F32),
        vmem((hpd, tokens, tokens), F32),
        vmem((hpd, 2, tokens, tokens), BF16),
        vmem((hpd, tokens + 8, HEAD_DIM), F32),
        vmem((hpd, 32, tokens + LANES), F32),
        vmem((hpd, HEAD_DIM, tokens), F32),
        vmem((groups, hpd, 8, 2 * LANES), F32),
        vmem((members, hpd, 8, 2 * LANES), F32),
        dma((3, hpd, members)),
        dma((3, hpd, members)),
        dma((2, hpd, members)),
        dma((2, hpd)),
        dma((2, 2, hpd, reach + 1)),
        dma((2, 2, hpd, reach + 1)),
        dma((2, hpd)),
        dma((2, hpd)),
        dma((2, hpd, members)),
        dma((2, hpd, members)),
        dma((groups,)),
        dma((groups,)),
        dma((members,)),
        dma((members,)),
        dma((2, hpd)),
    ]
    spec = pl.BlockSpec(memory_space=pltpu.VMEM)
    returned = (members, hpd, rows, HEAD_DIM), (members, hpd, 32, rows), (members, hpd, 8, 2 * LANES)
    anywhere = pl.BlockSpec(memory_space=pl.ANY)
    values, columns, taps = pl.pallas_call(
        functools.partial(kernel, sub, side, groups, reach, "seq", "head"),
        out_shape=tuple(jax.ShapeDtypeStruct(shape, F32) for shape in returned),
        in_specs=[pl.BlockSpec(memory_space=pltpu.SMEM), spec, spec, spec],
        out_specs=(anywhere, anywhere, spec),
        scratch_shapes=scratch,
        compiler_params=pltpu.CompilerParams(
            collective_id=0, has_side_effects=True, vmem_limit_bytes=60 * 1024 * 1024
        ),
        name="layer_backward",
    )(doc_lengths, projected, out_grads, conv_weight)
    pairs = members // 2
    return pl.pallas_call(
        functools.partial(unpack, hpd),
        out_shape=(
            jax.ShapeDtypeStruct(projected.shape, F32),
            jax.ShapeDtypeStruct(conv_weight.shape, F32),
        ),
        in_specs=[anywhere, anywhere, spec],
        out_specs=(anywhere, spec),
        scratch_shapes=[
            vmem(returned[0], F32),
            vmem(returned[1], F32),
            vmem(projected.shape, F32),
            dma((pairs,)),
            dma((pairs,)),
            dma((pairs,)),
        ],
        compiler_params=pltpu.CompilerParams(vmem_limit_bytes=60 * 1024 * 1024),
        name="unpack_heads",
    )(values, columns, taps)


def solution(mesh):
    side = mesh.shape["head"]
    sub = max(1, MEMBERS // side)
    groups = mesh.shape["seq"] // sub
    return jax.shard_map(
        functools.partial(on_device, sub, side, groups),
        mesh=mesh,
        in_specs=(P(("seq", "head"), None), P(("seq", "head"), None), P(), P()),
        out_specs=(P(("seq", "head"), None), P()),
        check_vma=False,
    )
```
